32 devices in a mesh: groups: 2 (over y), ctx: 4 (over z), chan: 2 (over x), grp: 2 (over core).
Axes of the slice: x: 2, y: 2, z: 4, core: 2. Of those that a mesh axis runs over, the one named last changes fastest.
Arguments:
- events: bfloat16 [4, 1024, 2048], P('groups', 'ctx', 'chan'), parts along dimension 0, may hold values from -6 to 6
- gap_bins: int32 [4, 1024], P('groups', 'ctx'), parts along dimension 0, may hold values from 0 to 63
- lengths: int32 [4], P('groups'), parts along dimension 0, may hold values from 128 to 1024, as said below
- gap_table: float32 [64], replicated, may hold values from 0.5 to 1024, as said below
- decay_rate: float32 [2048], P(('chan', 'grp')), may hold values from 0 to 1, as said below
- frequency: float32 [2048], P(('chan', 'grp')), may hold values from -3.140625 to 3.140625
- in_proj: bfloat16 [2048, 2, 2048], P(None, None, ('chan', 'grp')), may hold values from -0.125 to 0.125
- out_proj: bfloat16 [2, 2048, 2048], P(None, ('chan', 'grp')), may hold values from -0.09375 to 0.09375
- skip_gain: float32 [2048], P(('chan', 'grp')), may hold values from -4 to 4
Outputs:
- layer_out: bfloat16 [4, 1024, 2048], P('groups', 'ctx', ('chan', 'grp')), parts along dimension 0
The draws below stay inside these ranges and needn't reach their ends.
There are 2 independent parts, one for each index of `groups`. The reference program is written for one: setup_inputs(seed, part) draws one part's arguments, and reference() takes and returns one part's arrays. A program takes and returns all parts, laid end to end along the dimension named above; an argument that names none is the same for every part. Nothing has to cross between parts.
Inputs may be any that keep to these rules, and one draw needn't show every extreme that they name: `lengths`: some user has 1024. `gap_table`: positive. `decay_rate`: positive.
All inputs are finite; a program needn't handle non-finite values.
Results may differ from the reference program's by a relative error of at most 0.0035.
Values may be sent and summed in bfloat16 or wider, within the bound.
No kernel may reach another device: no remote copies, remote signals or barrier semaphores. Data moves between devices by JAX's collectives and lax.ppermute only.
A program may use at most 128 MiB of HBM per device.

```python
import math
import jax
import jax.numpy as jnp
from jax import lax

H = 2048
P_SIZE = 2048
GAP_TABLE_COUNT = 64
USERS = 2
LEN = 1024


def draw_gap_bins(key, part):
    first_key, second_key = jax.random.split(jax.random.fold_in(key, 11))
    shared_factor = jax.random.randint(first_key, (USERS, LEN), 0, GAP_TABLE_COUNT - 1)
    bin_locations = jax.random.randint(second_key, (USERS, 4), 0, LEN)
    target_positions = jnp.arange(LEN, dtype=jnp.int32)
    event_cluster = jnp.any(target_positions[None, :, None] == bin_locations[:, None, :], axis=-1)
    return jnp.where(event_cluster, GAP_TABLE_COUNT - 1, shared_factor).astype(jnp.int32)


def draw_lengths(key, part):
    first_key, second_key = jax.random.split(jax.random.fold_in(key, 23))
    drawn = jax.random.randint(first_key, (USERS,), LEN // 8, LEN + 1)
    longest = jax.random.randint(second_key, (), 0, USERS)
    users_idx = jnp.arange(USERS, dtype=jnp.int32)
    drawn = jnp.where(users_idx == longest, LEN, drawn)
    return drawn.astype(jnp.int32)


def draw_gap_table(key, part):
    first_key, second_key = jax.random.split(jax.random.fold_in(key, 37))
    shared_factor = jnp.exp(jax.random.uniform(first_key, (GAP_TABLE_COUNT,), jnp.float32, math.log(0.5), math.log(2.0)))
    largest = LEN / 4.0 * (1.0 + 0.5 * jax.random.uniform(second_key, (), jnp.float32))
    target_positions = jnp.arange(GAP_TABLE_COUNT, dtype=jnp.int32)
    return jnp.where(target_positions == GAP_TABLE_COUNT - 1, largest, shared_factor).astype(jnp.float32)


def draw_decay_rate(key, part):
    first_key = jax.random.fold_in(jax.random.fold_in(key, 53), 0)
    lowest = math.log(0.02 / LEN)
    highest = math.log(0.05)
    rates = jnp.exp(jax.random.uniform(first_key, (P_SIZE,), jnp.float32, lowest, highest))
    return rates.astype(jnp.float32)


def level_of(own_key, dims, shards, least, top_value):
    def one(axis_at, parts):
        heights = jax.random.uniform(jax.random.fold_in(jax.random.fold_in(own_key, 6), axis_at), (parts,), jnp.float32, least / len(shards), top_value / len(shards))
        return jnp.repeat(jnp.exp(heights), dims[axis_at] // parts).reshape((-1,) + (1,) * (len(dims) - axis_at - 1))

    level = one(*shards[0])
    for cut in shards[1:]:
        level = level * one(*cut)
    return level


def normal_values(rng, dims, scale, reach, cuts=(), kind=jnp.bfloat16):
    values = scale * jax.random.normal(rng, dims, jnp.float32)
    if cuts:
        values = values * level_of(rng, dims, cuts, -0.22, 0.18)
    return jnp.clip(values, -reach, reach).astype(kind)


def setup_inputs(seed: int = 0, part: int = 0) -> dict:
    key_list = jax.random.split(jax.random.key(seed), 10)
    own_keys = jax.random.split(jax.random.fold_in(key_list[9], part), 10)
    events = normal_values(own_keys[0], (USERS, LEN, H), 1.0, 6.0, ((1, 4), (2, 2)))
    gap_bins = draw_gap_bins(jax.random.fold_in(jax.random.fold_in(key_list[9], part), 71), part)
    lengths = draw_lengths(jax.random.fold_in(jax.random.fold_in(key_list[9], part), 71), part)
    gap_table = draw_gap_table(jax.random.fold_in(key_list[9], 71), part)
    decay_rate = draw_decay_rate(jax.random.fold_in(key_list[9], 71), part)
    frequency = jnp.clip(jax.random.uniform(key_list[5], (P_SIZE,), jnp.float32, -3.140625, 3.140625), -3.140625, 3.140625)
    in_proj = normal_values(key_list[6], (H, 2, P_SIZE), H ** -0.5, 0.125, ((2, 4),))
    out_proj = normal_values(key_list[7], (2, P_SIZE, H), (2 * P_SIZE) ** -0.5, 0.09375, ((1, 4),))
    skip_gain = normal_values(key_list[8], (H,), 1.0, 4.0, ((0, 4),), jnp.float32)
    return dict(events=events, gap_bins=gap_bins, lengths=lengths, gap_table=gap_table, decay_rate=decay_rate, frequency=frequency, in_proj=in_proj, out_proj=out_proj, skip_gain=skip_gain)


def reference(events, gap_bins, lengths, gap_table, decay_rate, frequency, in_proj, out_proj, skip_gain):
    gaps = gap_table[gap_bins]
    drive = jnp.einsum('ulh,hcp->ulcp', events.astype(jnp.float32), in_proj.astype(jnp.float32))
    scaled = gaps[..., None] * decay_rate
    magnitude = jnp.exp(-scaled)
    turned = gaps[..., None] * frequency
    decay_re = magnitude * jnp.cos(turned)
    decay_im = magnitude * jnp.sin(turned)
    norm_in = jnp.sqrt(-jnp.expm1(-2.0 * scaled))
    drive_re = norm_in * drive[:, :, 0]
    drive_im = norm_in * drive[:, :, 1]

    def advance(carry, inputs):
        state_re, state_im = carry
        mult_re, mult_im, add_re, added_imaginary = inputs
        next_re = mult_re * state_re - mult_im * state_im + add_re
        next_im = mult_re * state_im + mult_im * state_re + added_imaginary
        return ((next_re, next_im), (next_re, next_im))
    start = (jnp.zeros((USERS, P_SIZE), jnp.float32), jnp.zeros((USERS, P_SIZE), jnp.float32))
    moved = tuple((jnp.moveaxis(item, 1, 0) for item in (decay_re, decay_im, drive_re, drive_im)))
    _, (seq_re, seq_im) = lax.scan(advance, start, moved)
    states = jnp.stack([jnp.moveaxis(seq_re, 0, 1), jnp.moveaxis(seq_im, 0, 1)], 2).astype(jnp.bfloat16)
    mixed = jnp.einsum('ulcp,cph->ulh', states.astype(jnp.float32), out_proj.astype(jnp.float32))
    before = mixed + skip_gain * events.astype(jnp.float32)
    result = jax.nn.gelu(before)
    target_positions = jnp.arange(LEN, dtype=jnp.int32)
    valid = target_positions[None, :] < lengths[:, None]
    return jnp.where(valid[..., None], result, 0.0).astype(jnp.bfloat16)
```

```python
import functools

import jax
import jax.numpy as jnp
from jax import lax
from jax.experimental import pallas as pl
from jax.experimental.pallas import tpu as pltpu
from jax.sharding import PartitionSpec as P

F32 = jnp.float32
BF16 = jnp.bfloat16
SEGS = 8
VMEM = 48 * 1024 * 1024


def dot(a, b):
    return jnp.dot(a, b, preferred_element_type=F32)


def cmul(ar, ai, br, bi):
    return ar * br - ai * bi, ar * bi + ai * br


def order_matrix(tokens):
    steps = tokens // SEGS
    r = lax.broadcasted_iota(jnp.int32, (tokens, tokens), 0)
    t = lax.broadcasted_iota(jnp.int32, (tokens, tokens), 1)
    return (t == (r % SEGS) * steps + r // SEGS).astype(F32).astype(BF16)


def run_starts(ar, ai, er, ei):
    cr, ci = jnp.zeros_like(er[:1]), jnp.zeros_like(ei[:1])
    rows_r, rows_i = [], []
    for i in range(SEGS):
        rows_r.append(cr)
        rows_i.append(ci)
        xr, xi = cmul(ar[i : i + 1], ai[i : i + 1], cr, ci)
        cr, ci = xr + er[i : i + 1], xi + ei[i : i + 1]
    return jnp.concatenate(rows_r, 0), jnp.concatenate(rows_i, 0), cr, ci


def run_products(ar, ai):
    cr, ci = jnp.ones_like(ar[:1]), jnp.zeros_like(ai[:1])
    rows_r, rows_i = [], []
    for i in range(SEGS):
        rows_r.append(cr)
        rows_i.append(ci)
        cr, ci = cmul(ar[i : i + 1], ai[i : i + 1], cr, ci)
    return jnp.concatenate(rows_r, 0), jnp.concatenate(rows_i, 0), cr, ci


def decay_kernel(users, tokens, ids, bins, table, dec, cum, prod, runs):
    grp = ids[1]
    half = pl.program_id(0)
    place = jnp.where(half == 0, grp, 1 - grp)
    count = table.shape[2]
    order = order_matrix(tokens)
    steps = tokens // SEGS
    pieces = []
    for k in range(3):
        full = table[0, k]
        high = full.astype(BF16)
        rest = full - high.astype(F32)
        mid = rest.astype(BF16)
        low = (rest - mid.astype(F32)).astype(BF16)
        pieces.append((high, mid, low))
    for u in range(users):
        row = bins[u : u + 1, pl.ds(pl.multiple_of(grp * tokens, tokens), tokens)]
        hit = (lax.broadcasted_iota(jnp.int32, (count, tokens), 0) == row).astype(F32).astype(BF16)
        pick = lax.dot_general(
            order, hit, (((1,), (1,)), ((), ())), preferred_element_type=F32
        ).astype(BF16)
        for k in range(3):
            high, mid, low = pieces[k]
            dec[k, 0, u * tokens : (u + 1) * tokens, :] = (
                dot(pick, high) + dot(pick, mid)
            ) + dot(pick, low)
        base = u * tokens

        def at(s):
            rows = slice(base + s * SEGS, base + (s + 1) * SEGS)
            return dec[0, 0, rows, :], dec[1, 0, rows, :]

        pr, pi = at(0)
        for s in range(1, steps):
            dr, di = at(s)
            pr, pi = cmul(dr, di, pr, pi)
        runs[0, 0, u * SEGS : (u + 1) * SEGS, :] = pr
        runs[1, 0, u * SEGS : (u + 1) * SEGS, :] = pi
        cr, ci, tr, ti = run_products(pr, pi)
        prod[place, u : u + 1, :] = tr
        prod[2 + place, u : u + 1, :] = ti
        for s in range(steps):
            dr, di = at(s)
            cr, ci = cmul(dr, di, cr, ci)
            rows = slice(base + s * SEGS, base + (s + 1) * SEGS)
            cum[0, 0, rows, :] = cr
            cum[1, 0, rows, :] = ci


def weight_kernel(xor, ids, prods, out):
    me = ids[2]
    blocks = prods.shape[0]
    half = prods.shape[1] // 2
    one = jnp.ones(prods.shape[2:], F32)
    zero = jnp.zeros(prods.shape[2:], F32)

    def step(n, carry):
        j = blocks - 1 - n
        before = j < me
        new = []
        for h in range(half):
            r, i = carry[2 * h], carry[2 * h + 1]
            where = (j ^ me) if xor else j
            out[where, h] = jnp.where(before, r, 0.0)
            out[where, half + h] = jnp.where(before, i, 0.0)
            xr, xi = cmul(prods[j, h], prods[j, half + h], r, i)
            new += [jnp.where(before, xr, r), jnp.where(before, xi, i)]
        return tuple(new)

    lax.fori_loop(0, blocks, step, (one, zero) * half)


def into_order(users, tokens, source, target):
    order = order_matrix(tokens)
    for u in range(users):
        target[u * tokens : (u + 1) * tokens, :] = dot(order, source[u]).astype(BF16)


def own_kernel(users, tokens, ids, events, w_own, w_oth, out, rows):
    @pl.when(pl.program_id(0) == 0)
    def _():
        into_order(users, tokens, events, rows)

    for h, w in enumerate((w_own, w_oth)):
        for c in range(2):
            out[c, h] = dot(rows[...], w[c])


def scan_kernel(users, tokens, peers, ids, *refs):
    events = refs[:peers]
    weights = refs[peers : 3 * peers]
    part, dec, runs, state, ends, rows, drive = refs[3 * peers :]
    grp = ids[1]
    steps = tokens // SEGS

    @pl.when(pl.program_id(0) == 0)
    def _():
        for n in range(peers):
            into_order(users, tokens, events[n], rows.at[n])

    for h in range(2):
        place = grp if h == 0 else 1 - grp
        for c in range(2):
            total = part[c, h]
            for n in range(peers):
                total = total + dot(rows[n], weights[2 * n + h][c])
            drive[c] = dec[2, h] * total
        for u in range(users):
            base = u * tokens

            def at(s):
                sl = slice(base + s * SEGS, base + (s + 1) * SEGS)
                return dec[0, h, sl, :], dec[1, h, sl, :], drive[0, sl, :], drive[1, sl, :]

            _, _, sr, si = at(0)
            for s in range(1, steps):
                dr, di, vr, vi = at(s)
                xr, xi = cmul(dr, di, sr, si)
                sr, si = xr + vr, xi + vi
            ar = runs[0, h, u * SEGS : (u + 1) * SEGS, :]
            ai = runs[1, h, u * SEGS : (u + 1) * SEGS, :]
            sr, si, er, ei = run_starts(ar, ai, sr, si)
            ends[place, u : u + 1, :] = er
            ends[2 + place, u : u + 1, :] = ei
            for s in range(steps):
                dr, di, vr, vi = at(s)
                xr, xi = cmul(dr, di, sr, si)
                sr, si = xr + vr, xi + vi
                sl = slice(base + s * SEGS, base + (s + 1) * SEGS)
                state[0, h, sl, :] = sr
                state[1, h, sl, :] = si


def carry_kernel(users, tokens, firsts, ids, *refs):
    given = refs[: len(firsts)]
    weights, state, cum, out = refs[len(firsts) :]
    grp = ids[1]
    order = order_matrix(tokens)
    for h in range(2):
        place = grp if h == 0 else 1 - grp
        cr = jnp.zeros(weights.shape[2:], F32)
        ci = jnp.zeros(weights.shape[2:], F32)
        for first, ref in zip(firsts, given):
            for n in range(ref.shape[0]):
                xr, xi = cmul(
                    weights[first + n, place],
                    weights[first + n, 2 + place],
                    ref[n, place],
                    ref[n, 2 + place],
                )
                cr, ci = cr + xr, ci + xi
        for u in range(users):
            sl = slice(u * tokens, (u + 1) * tokens)
            xr, xi = cmul(cum[0, h, sl, :], cum[1, h, sl, :], cr[u : u + 1], ci[u : u + 1])
            for c, value in ((0, state[0, h, sl, :] + xr), (1, state[1, h, sl, :] + xi)):
                moved = lax.dot_general(
                    order, value.astype(BF16), (((0,), (0,)), ((), ())), preferred_element_type=F32
                )
                out[c, h, sl, :] = moved.astype(BF16)


def mix_kernel(ids, states, w_own, w_oth, out):
    total = None
    for h, w in enumerate((w_own, w_oth)):
        for c in range(2):
            term = dot(states[c, h], w[c])
            total = term if total is None else total + term
    out[...] = total.astype(out.dtype)


def final_kernel(users, tokens, same, cross, ids, lengths, *refs):
    mine, other = refs[:same], refs[same : same + cross]
    events, gain, out = refs[same + cross :]
    grp = ids[1]
    for u in range(users):
        sl = slice(u * tokens, (u + 1) * tokens)
        for where, parts in ((grp, mine), (1 - grp, other)):
            start = pl.multiple_of(where * tokens, tokens)
            total = parts[0][sl, :].astype(F32)
            for part in parts[1:]:
                total = total + part[sl, :].astype(F32)
            own = events[u, pl.ds(start, tokens), :].astype(F32)
            result = jax.nn.gelu(total + gain[...] * own)
            position = (
                ids[3] + start + lax.broadcasted_iota(jnp.int32, result.shape, 0)
            )
            result = jnp.where(position < lengths[u], result, 0.0)
            out[u, pl.ds(start, tokens), :] = result.astype(BF16)


def call(body, name, ids, args, in_specs, out_shape, out_specs, grid=(1,), scratch=(), flops=0, bytes_=0):
    return pl.pallas_call(
        body,
        name=name,
        out_shape=out_shape,
        grid_spec=pltpu.PrefetchScalarGridSpec(
            num_scalar_prefetch=len(ids),
            grid=grid,
            in_specs=in_specs,
            out_specs=out_specs,
            scratch_shapes=list(scratch),
        ),
        compiler_params=pltpu.CompilerParams(vmem_limit_bytes=VMEM),
        cost_estimate=pl.CostEstimate(flops=flops, bytes_accessed=bytes_, transcendentals=0),
    )(*ids, *args)


def whole(array):
    rank = array.ndim
    return pl.BlockSpec(array.shape, lambda *_: (0,) * rank)


def shape(dims, kind):
    return jax.ShapeDtypeStruct(dims, kind)


def local(
    events, gap_bins, lengths, gap_table, decay_rate, frequency, in_proj, out_proj, skip_gain
):
    users, seg_rows, width = events.shape
    model_width = in_proj.shape[0]
    q = decay_rate.shape[0]
    grps, chans, ctxs = (lax.axis_size(a) for a in ("grp", "chan", "ctx"))
    assert grps == 2
    tokens = seg_rows // grps
    rows = users * tokens
    count = gap_table.shape[0]
    devices, blocks = chans * grps, ctxs * grps
    part_width = model_width // devices

    chan, grp, ctx = (lax.axis_index(a) for a in ("chan", "grp", "ctx"))
    ids = jnp.stack(
        [chan, grp, ctx * grps + grp, ctx * seg_rows, chan * grps + grp]
    ).astype(jnp.int32)

    def swap(array, axes, size, k):
        return lax.ppermute(array, axes, [(i, i ^ k) for i in range(size)])

    own_rows = lax.dynamic_slice_in_dim(events, grp * tokens, tokens, 1)
    peer_rows = [swap(own_rows, "chan", chans, k) for k in range(1, chans)]

    w_own = jnp.transpose(in_proj, (1, 0, 2))
    w_oth = swap(w_own, "grp", grps, 1)
    rates = jnp.stack([decay_rate, frequency])
    rates_oth = swap(rates, "grp", grps, 1)
    o_oth = swap(out_proj, "grp", grps, 1)

    both = jnp.stack([rates, rates_oth])
    scaled = gap_table[None, :, None] * both[:, 0][:, None, :]
    turned = gap_table[None, :, None] * both[:, 1][:, None, :]
    magnitude = jnp.exp(-scaled)
    table = jnp.stack(
        [
            magnitude * jnp.cos(turned),
            magnitude * jnp.sin(turned),
            jnp.sqrt(-jnp.expm1(-2.0 * scaled)),
        ],
        1,
    )

    dec, cum, prod, runs = call(
        functools.partial(decay_kernel, users, tokens),
        "decays",
        (ids,),
        (gap_bins, table),
        [
            whole(gap_bins),
            pl.BlockSpec((1, 3, count, q), lambda i, ids: (i, 0, 0, 0)),
        ],
        (
            shape((3, 2, rows, q), F32),
            shape((2, 2, rows, q), F32),
            shape((4, users, q), F32),
            shape((2, 2, users * SEGS, q), F32),
        ),
        (
            pl.BlockSpec((3, 1, rows, q), lambda i, ids: (0, i, 0, 0)),
            pl.BlockSpec((2, 1, rows, q), lambda i, ids: (0, i, 0, 0)),
            pl.BlockSpec((4, users, q), lambda i, ids: (0, 0, 0)),
            pl.BlockSpec((2, 1, users * SEGS, q), lambda i, ids: (0, i, 0, 0)),
        ),
        grid=(2,),
        flops=2 * rows * q * 2 * 9 * count,
        bytes_=5 * 2 * rows * q * 4,
    )

    prods = lax.all_gather(prod, ("ctx", "grp"))
    xor = blocks <= 8
    weights = call(
        functools.partial(weight_kernel, xor),
        "between",
        (ids,),
        (prods,),
        [whole(prods)],
        shape(prods.shape, F32),
        whole(prods),
        bytes_=2 * prods.size * 4,
    )

    step = min(q, 256)
    part = call(
        functools.partial(own_kernel, users, tokens),
        "own_drive",
        (ids,),
        (own_rows, w_own, w_oth),
        [whole(own_rows)]
        + [pl.BlockSpec((2, width, step), lambda i, ids: (0, ids[0], i))] * 2,
        shape((2, 2, rows, q), F32),
        pl.BlockSpec((2, 2, rows, step), lambda i, ids: (0, 0, 0, i)),
        grid=(q // step,),
        scratch=[pltpu.VMEM((rows, width), BF16)],
        flops=2 * rows * width * 4 * q,
        bytes_=4 * width * q * 2 + 4 * rows * q * 4,
    )

    peers = chans - 1
    w_specs = []
    for k in range(1, chans):
        w_specs += [
            pl.BlockSpec((2, width, step), lambda i, ids, k=k: (0, ids[0] ^ k, i))
        ] * 2
    state, ends = call(
        functools.partial(scan_kernel, users, tokens, peers),
        "drive_scan",
        (ids,),
        (*peer_rows, *((w_own, w_oth) * peers), part, dec, runs),
        [whole(p) for p in peer_rows]
        + w_specs
        + [
            pl.BlockSpec((2, 2, rows, step), lambda i, ids: (0, 0, 0, i)),
            pl.BlockSpec((3, 2, rows, step), lambda i, ids: (0, 0, 0, i)),
            pl.BlockSpec((2, 2, users * SEGS, step), lambda i, ids: (0, 0, 0, i)),
        ],
        (shape((2, 2, rows, q), F32), shape((4, users, q), F32)),
        (
            pl.BlockSpec((2, 2, rows, step), lambda i, ids: (0, 0, 0, i)),
            pl.BlockSpec((4, users, step), lambda i, ids: (0, 0, i)),
        ),
        grid=(q // step,),
        scratch=[
            pltpu.VMEM((peers, rows, width), BF16),
            pltpu.VMEM((2, rows, step), F32),
        ],
        flops=2 * rows * width * 4 * q * peers,
        bytes_=4 * width * q * 2 * peers + 4 * rows * q * 12,
    )

    if xor:
        given = [swap(ends, ("ctx", "grp"), blocks, k)[None] for k in range(1, blocks)]
        firsts = tuple(range(1, blocks))
    else:
        given = [lax.all_gather(ends, ("ctx", "grp"))]
        firsts = (0,)

    states = call(
        functools.partial(carry_kernel, users, tokens, firsts),
        "carry_in",
        (ids,),
        (*given, weights, state, cum),
        [whole(g) for g in given] + [whole(weights), whole(state), whole(cum)],
        shape((2, 2, rows, q), BF16),
        pl.BlockSpec((2, 2, rows, q), lambda i, ids: (0, 0, 0, 0)),
        flops=2 * rows * tokens * 4 * q,
        bytes_=rows * q * 4 * 10,
    )

    cols = min(part_width, 256)

    def mixed(d, kind):
        def spec(i, ids):
            return (0, 0, (ids[4] ^ d) * (part_width // cols) + i)

        return call(
            mix_kernel,
            "mix_%d" % d,
            (ids,),
            (states, out_proj, o_oth),
            [whole(states)] + [pl.BlockSpec((2, q, cols), spec)] * 2,
            shape((rows, part_width), kind),
            pl.BlockSpec((rows, cols), lambda i, ids: (0, i)),
            grid=(part_width // cols,),
            flops=2 * rows * part_width * 4 * q,
            bytes_=4 * q * part_width * 2 + rows * part_width * 2 + 4 * rows * q * 2,
        )

    order = list(range(2, devices)) + [1]
    received = {
        d: swap(mixed(d, F32 if d == 1 else BF16), ("chan", "grp"), devices, d) for d in order
    }
    received[0] = mixed(0, F32)
    same = [received[d] for d in range(0, devices, 2)]
    cross = [received[d] for d in range(1, devices, 2)]

    own_events = lax.dynamic_slice_in_dim(events, grp * part_width, part_width, 2)
    gain = skip_gain[None]
    return call(
        functools.partial(final_kernel, users, tokens, len(same), len(cross)),
        "final",
        (ids, lengths),
        (*same, *cross, own_events, gain),
        [whole(a) for a in (*same, *cross, own_events, gain)],
        shape((users, seg_rows, part_width), BF16),
        pl.BlockSpec((users, seg_rows, part_width), lambda i, ids, lengths: (0, 0, 0)),
        bytes_=rows * part_width * 12,
    )


def solution(mesh):
    return jax.shard_map(
        local,
        mesh=mesh,
        in_specs=(
            P("groups", "ctx", "chan"),
            P("groups", "ctx"),
            P("groups"),
            P(),
            P(("chan", "grp")),
            P(("chan", "grp")),
            P(None, None, ("chan", "grp")),
            P(None, ("chan", "grp"), None),
            P(("chan", "grp")),
        ),
        out_specs=P("groups", "ctx", ("chan", "grp")),
        check_vma=False,
    )
```

```python
import functools

import jax
import jax.numpy as jnp
from jax import lax
from jax.experimental import pallas as pl
from jax.experimental.layout import Layout, with_layout_constraint
from jax.experimental.pallas import tpu as pltpu
from jax.sharding import PartitionSpec as P

F32 = jnp.float32
BF16 = jnp.bfloat16
SEGS = 8
VMEM = 16 * 1024 * 1024
HERE = pl.BlockSpec(memory_space=pltpu.VMEM)


def dot(a, b):
    return jnp.dot(a, b, preferred_element_type=F32)


def cmul(ar, ai, br, bi):
    return ar * br - ai * bi, ar * bi + ai * br


def order_matrix(tokens):
    steps = tokens // SEGS
    r = lax.broadcasted_iota(jnp.int32, (tokens, tokens), 0)
    t = lax.broadcasted_iota(jnp.int32, (tokens, tokens), 1)
    return (t == (r % SEGS) * steps + r // SEGS).astype(F32).astype(BF16)


def run_starts(ar, ai, er, ei):
    cr, ci = jnp.zeros_like(er[:1]), jnp.zeros_like(ei[:1])
    rows_r, rows_i = [], []
    for i in range(SEGS):
        rows_r.append(cr)
        rows_i.append(ci)
        xr, xi = cmul(ar[i : i + 1], ai[i : i + 1], cr, ci)
        cr, ci = xr + er[i : i + 1], xi + ei[i : i + 1]
    return jnp.concatenate(rows_r, 0), jnp.concatenate(rows_i, 0), cr, ci


def run_products(ar, ai):
    cr, ci = jnp.ones_like(ar[:1]), jnp.zeros_like(ai[:1])
    rows_r, rows_i = [], []
    for i in range(SEGS):
        rows_r.append(cr)
        rows_i.append(ci)
        cr, ci = cmul(ar[i : i + 1], ai[i : i + 1], cr, ci)
    return jnp.concatenate(rows_r, 0), jnp.concatenate(rows_i, 0), cr, ci


def decay_kernel(tokens, bins, table, dec, cum, prod, runs, later):
    grp = lax.axis_index("grp")
    users = bins.shape[0]
    count = table.shape[2]
    me = lax.axis_index("ctx") * lax.axis_size("grp") + grp
    for k in range(later.shape[0]):
        later[k] = jnp.full(later.shape[1:], (me >> k) & 1, jnp.int32)
    order = order_matrix(tokens)
    steps = tokens // SEGS
    picks = []
    for u in range(users):
        row = bins[u : u + 1, pl.ds(pl.multiple_of(grp * tokens, tokens), tokens)]
        hit = (lax.broadcasted_iota(jnp.int32, (count, tokens), 0) == row).astype(F32).astype(BF16)
        picks.append(
            lax.dot_general(
                order, hit, (((1,), (1,)), ((), ())), preferred_element_type=F32
            ).astype(BF16)
        )
    pick = jnp.concatenate(picks, 0)
    pick = jnp.concatenate([pick] * 3, 1)
    for h in range(2):
        place = grp if h == 0 else 1 - grp
        for k in range(3):
            full = table[h, k]
            high = full.astype(BF16)
            rest = full - high.astype(F32)
            mid = rest.astype(BF16)
            low = (rest - mid.astype(F32)).astype(BF16)
            dec[k, h] = dot(pick, jnp.concatenate([high, mid, low], 0))
        for u in range(users):
            base = u * tokens

            def at(s):
                rows = slice(base + s * SEGS, base + (s + 1) * SEGS)
                return dec[0, h, rows, :], dec[1, h, rows, :]

            pr, pi = at(0)
            for s in range(1, steps):
                dr, di = at(s)
                pr, pi = cmul(dr, di, pr, pi)
            runs[0, h, u * SEGS : (u + 1) * SEGS, :] = pr
            runs[1, h, u * SEGS : (u + 1) * SEGS, :] = pi
            cr, ci, tr, ti = run_products(pr, pi)
            prod[place, u : u + 1, :] = tr
            prod[2 + place, u : u + 1, :] = ti
            for s in range(steps):
                dr, di = at(s)
                cr, ci = cmul(dr, di, cr, ci)
                rows = slice(base + s * SEGS, base + (s + 1) * SEGS)
                cum[0, h, rows, :] = cr
                cum[1, h, rows, :] = ci


def own_kernel(tokens, events, w, out):
    chan = lax.axis_index("chan")
    users, _, width = events.shape
    order = order_matrix(tokens)
    rows = jnp.concatenate([dot(order, events[u]).astype(BF16) for u in range(users)], 0)
    start = pl.ds(pl.multiple_of(chan * width, width), width)
    for c in range(2):
        out[c] = dot(rows, w[c, start, :])


def scan_kernel(tokens, peers, *refs):
    events = refs[:peers]
    weights = refs[peers : peers + 2]
    parts = refs[peers + 2 : peers + 4]
    dec, runs, state, ends, drive = refs[peers + 4 :]
    chan, grp = lax.axis_index("chan"), lax.axis_index("grp")
    users, _, width = events[0].shape
    steps = tokens // SEGS
    order = order_matrix(tokens)
    rows = [
        jnp.concatenate([dot(order, ev[u]).astype(BF16) for u in range(users)], 0) for ev in events
    ]
    for h in range(2):
        place = grp if h == 0 else 1 - grp
        for c in range(2):
            total = parts[h][c]
            for n in range(peers):
                start = pl.multiple_of((chan ^ (n + 1)) * width, width)
                total = total + dot(rows[n], weights[h][c, pl.ds(start, width), :])
            drive[c] = dec[2, h] * total
        for u in range(users):
            base = u * tokens

            def at(s):
                sl = slice(base + s * SEGS, base + (s + 1) * SEGS)
                return dec[0, h, sl, :], dec[1, h, sl, :], drive[0, sl, :], drive[1, sl, :]

            _, _, sr, si = at(0)
            for s in range(1, steps):
                dr, di, vr, vi = at(s)
                xr, xi = cmul(dr, di, sr, si)
                sr, si = xr + vr, xi + vi
            ar = runs[0, h, u * SEGS : (u + 1) * SEGS, :]
            ai = runs[1, h, u * SEGS : (u + 1) * SEGS, :]
            sr, si, er, ei = run_starts(ar, ai, sr, si)
            ends[place, u : u + 1, :] = er
            ends[2 + place, u : u + 1, :] = ei
            for s in range(steps):
                dr, di, vr, vi = at(s)
                xr, xi = cmul(dr, di, sr, si)
                sr, si = xr + vr, xi + vi
                sl = slice(base + s * SEGS, base + (s + 1) * SEGS)
                state[0, h, sl, :] = sr
                state[1, h, sl, :] = si


def carry_kernel(tokens, carry, state, cum, out):
    grp = lax.axis_index("grp")
    users = carry.shape[1]
    order = order_matrix(tokens)
    for h in range(2):
        place = grp if h == 0 else 1 - grp
        cr, ci = carry[place], carry[2 + place]
        for u in range(users):
            sl = slice(u * tokens, (u + 1) * tokens)
            xr, xi = cmul(cum[0, h, sl, :], cum[1, h, sl, :], cr[u : u + 1], ci[u : u + 1])
            for c, value in ((0, state[0, h, sl, :] + xr), (1, state[1, h, sl, :] + xi)):
                moved = lax.dot_general(
                    order, value.astype(BF16), (((0,), (0,)), ((), ())), preferred_element_type=F32
                )
                out[c, h, sl, :] = moved.astype(BF16)


def mix(d, states, w_own, w_oth, width):
    at = (lax.axis_index("chan") * lax.axis_size("grp") + lax.axis_index("grp")) ^ d
    cols = pl.ds(pl.multiple_of(at * width, width), width)
    total = None
    for h, w in enumerate((w_own, w_oth)):
        for c in range(2):
            term = dot(states[c, h], w[c, :, cols])
            total = term if total is None else total + term
    return total


def first_mix_kernel(tokens, d, carry, state, cum, w_own, w_oth, states, out):
    carry_kernel(tokens, carry, state, cum, states)
    out[...] = mix(d, states, w_own, w_oth, out.shape[1]).astype(out.dtype)


def mix_kernel(d, states, w_own, w_oth, out):
    out[...] = mix(d, states, w_own, w_oth, out.shape[1]).astype(out.dtype)


def hold_kernel(source, target, sem):
    copy = pltpu.make_async_copy(source, target, sem)
    copy.start()
    copy.wait()


def final_kernel(tokens, same, cross, lengths, *refs):
    mine, other = refs[:same], refs[same : same + cross]
    events, gain, out = refs[same + cross :]
    users, seg_rows, _ = out.shape
    grp = lax.axis_index("grp")
    first = lax.axis_index("ctx") * seg_rows
    for u in range(users):
        sl = slice(u * tokens, (u + 1) * tokens)
        for where, parts in ((grp, mine), (1 - grp, other)):
            start = pl.multiple_of(where * tokens, tokens)
            total = parts[0][sl, :].astype(F32)
            for part in parts[1:]:
                total = total + part[sl, :].astype(F32)
            own = events[u, pl.ds(start, tokens), :].astype(F32)
            result = jax.nn.gelu(total + gain[...] * own)
            position = first + start + lax.broadcasted_iota(jnp.int32, result.shape, 0)
            result = jnp.where(position < lengths[u], result, 0.0)
            out[u, pl.ds(start, tokens), :] = result.astype(BF16)


def call(body, name, args, out_shape, scratch=(), flops=0, bytes_=0, in_specs=None, out_specs=None):
    single = not isinstance(out_shape, tuple)
    return pl.pallas_call(
        body,
        name=name,
        out_shape=out_shape,
        in_specs=in_specs or [HERE] * len(args),
        out_specs=out_specs or (HERE if single else (HERE,) * len(out_shape)),
        scratch_shapes=list(scratch),
        compiler_params=pltpu.CompilerParams(vmem_limit_bytes=VMEM),
        cost_estimate=pl.CostEstimate(flops=flops, bytes_accessed=bytes_, transcendentals=0),
    )(*args)


def shape(dims, kind):
    return jax.ShapeDtypeStruct(dims, kind)


def join(first, second):
    ar, ai, br, bi = first[0][:2], first[0][2:], second[0][:2], second[0][2:]
    er, ei, fr, fi = first[1][:2], first[1][2:], second[1][:2], second[1][2:]
    pr, pi = cmul(br, bi, ar, ai)
    xr, xi = cmul(br, bi, er, ei)
    return jnp.concatenate([pr, pi]), jnp.concatenate([xr + fr, xi + fi])


def local(
    events, gap_bins, lengths, gap_table, decay_rate, frequency, in_proj, out_proj, skip_gain
):
    users, seg_rows, width = events.shape
    model_width = in_proj.shape[0]
    q = decay_rate.shape[0]
    grps, chans, ctxs = (lax.axis_size(a) for a in ("grp", "chan", "ctx"))
    assert grps == 2
    tokens = seg_rows // grps
    rows = users * tokens
    devices, blocks = chans * grps, ctxs * grps
    part_width = model_width // devices
    grp = lax.axis_index("grp")

    def swap(array, axes, size, k):
        return lax.ppermute(array, axes, [(i, i ^ k) for i in range(size)])

    own_rows = lax.dynamic_slice_in_dim(events, grp * tokens, tokens, 1)
    own_events = lax.dynamic_slice_in_dim(events, grp * part_width, part_width, 2)
    own_rows, own_events = lax.optimization_barrier((own_rows, own_events))
    peer_rows = [swap(own_rows, "chan", chans, k) for k in range(1, chans)]

    rates = jnp.stack([decay_rate, frequency])
    groups = lax.axis_size("groups")
    by = 3 if groups == 2 else 1
    stored = Layout((0, 1, 2))
    raw_oth = swap(with_layout_constraint(in_proj, stored), "grp", grps, 1)
    raw_oth = with_layout_constraint(raw_oth, stored)
    o_oth = swap(out_proj, "grp", grps, 1)
    w_own = jnp.transpose(in_proj, (1, 0, 2))
    w_oth = jnp.transpose(raw_oth, (1, 0, 2))

    parts = [
        call(
            functools.partial(own_kernel, tokens),
            "own_drive_%d" % h,
            (own_rows, w),
            shape((2, rows, q), F32),
            flops=2 * rows * width * 2 * q,
            bytes_=2 * width * q * 2 + 2 * rows * q * 4,
        )
        for h, w in enumerate((w_own, w_oth))
    ]

    rates_oth = swap(rates, ("groups", "grp"), groups * grps, by)
    rates_oth, _ = lax.optimization_barrier((rates_oth, parts[1]))
    both = jnp.stack([rates, rates_oth])
    scaled = gap_table[None, :, None] * both[:, 0][:, None, :]
    turned = gap_table[None, :, None] * both[:, 1][:, None, :]
    magnitude = jnp.exp(-scaled)
    table = jnp.stack(
        [
            magnitude * jnp.cos(turned),
            magnitude * jnp.sin(turned),
            jnp.sqrt(-jnp.expm1(-2.0 * scaled)),
        ],
        1,
    )

    rounds = blocks.bit_length() - 1
    dec, cum, prod, runs, later = call(
        functools.partial(decay_kernel, tokens),
        "decays",
        (gap_bins, table),
        (
            shape((3, 2, rows, q), F32),
            shape((2, 2, rows, q), F32),
            shape((4, users, q), F32),
            shape((2, 2, users * SEGS, q), F32),
            shape((rounds, users, q), jnp.int32),
        ),
        flops=2 * rows * q * 2 * 9 * gap_table.shape[0],
        bytes_=5 * 2 * rows * q * 4,
    )

    peers = chans - 1
    state, ends = call(
        functools.partial(scan_kernel, tokens, peers),
        "drive_scan",
        (*peer_rows, w_own, w_oth, *parts, dec, runs),
        (shape((2, 2, rows, q), F32), shape((4, users, q), F32)),
        scratch=[pltpu.VMEM((2, rows, q), F32)],
        flops=2 * rows * width * 4 * q * peers,
        bytes_=4 * width * q * 2 * peers + 4 * rows * q * 12,
    )

    o_oth = call(hold_kernel, "hold", (o_oth,), shape(o_oth.shape, BF16),
        scratch=[pltpu.SemaphoreType.DMA(())],
        in_specs=[pl.BlockSpec(memory_space=pl.ANY)],
        bytes_=4 * o_oth.size,
    )
    group = (prod, ends)
    before = (jnp.concatenate([jnp.ones_like(prod[:2]), jnp.zeros_like(prod[2:])]), jnp.zeros_like(ends))
    for k in range(rounds):
        theirs = swap(jnp.concatenate(group), ("ctx", "grp"), blocks, 1 << k)
        theirs = (theirs[:4], theirs[4:])
        second = later[k] > 0
        longer = join(theirs, before)
        before = tuple(jnp.where(second, a, b) for a, b in zip(longer, before))
        group = tuple(
            jnp.where(second, a, b) for a, b in zip(join(theirs, group), join(group, theirs))
        )
    carry = before[1]

    order = list(range(2, devices)) + [1]
    received = {}
    states, piece = call(
        functools.partial(first_mix_kernel, tokens, order[0]),
        "carry_mix",
        (carry, state, cum, out_proj, o_oth),
        (shape((2, 2, rows, q), BF16), shape((rows, part_width), BF16)),
        flops=2 * rows * part_width * 4 * q,
        bytes_=4 * q * part_width * 2 + 6 * rows * q * 4,
    )
    received[order[0]] = swap(piece, ("chan", "grp"), devices, order[0])
    for d in order[1:] + [0]:
        piece = call(
            functools.partial(mix_kernel, d),
            "mix_%d" % d,
            (states, out_proj, o_oth),
            shape((rows, part_width), F32 if d < 2 else BF16),
            flops=2 * rows * part_width * 4 * q,
            bytes_=4 * q * part_width * 2 + rows * part_width * 2 + 4 * rows * q * 2,
        )
        received[d] = swap(piece, ("chan", "grp"), devices, d) if d else piece
    same = [received[d] for d in range(0, devices, 2)]
    cross = [received[d] for d in range(1, devices, 2)]

    gain = skip_gain[None]
    given = (lengths, *same, *cross, own_events, gain)
    return call(
        functools.partial(final_kernel, tokens, len(same), len(cross)),
        "final",
        given,
        shape((users, seg_rows, part_width), BF16),
        in_specs=[pl.BlockSpec(memory_space=pltpu.SMEM)] + [HERE] * (len(given) - 1),
        out_specs=HERE,
        bytes_=rows * part_width * 12,
    )


def solution(mesh):
    return jax.shard_map(
        local,
        mesh=mesh,
        in_specs=(
            P("groups", "ctx", "chan"),
            P("groups", "ctx"),
            P("groups"),
            P(),
            P(("chan", "grp")),
            P(("chan", "grp")),
            P(None, None, ("chan", "grp")),
            P(None, ("chan", "grp"), None),
            P(("chan", "grp")),
        ),
        out_specs=P("groups", "ctx", ("chan", "grp")),
        check_vma=False,
    )
```

```python
import functools

import jax
import jax.numpy as jnp
from jax import lax
from jax.experimental import pallas as pl
from jax.experimental.layout import Layout, with_layout_constraint
from jax.experimental.pallas import tpu as pltpu
from jax.sharding import PartitionSpec as P

F32 = jnp.float32
BF16 = jnp.bfloat16
SEGS = 8
VMEM = 16 * 1024 * 1024
HERE = pl.BlockSpec(memory_space=pltpu.VMEM)


def dot(a, b):
    return jnp.dot(a, b, preferred_element_type=F32)


def cmul(ar, ai, br, bi):
    return ar * br - ai * bi, ar * bi + ai * br


def order_matrix(tokens):
    steps = tokens // SEGS
    r = lax.broadcasted_iota(jnp.int32, (tokens, tokens), 0)
    t = lax.broadcasted_iota(jnp.int32, (tokens, tokens), 1)
    return (t == (r % SEGS) * steps + r // SEGS).astype(F32).astype(BF16)


def run_starts(ar, ai, er, ei):
    cr, ci = jnp.zeros_like(er[:1]), jnp.zeros_like(ei[:1])
    rows_r, rows_i = [], []
    for i in range(SEGS):
        rows_r.append(cr)
        rows_i.append(ci)
        xr, xi = cmul(ar[i : i + 1], ai[i : i + 1], cr, ci)
        cr, ci = xr + er[i : i + 1], xi + ei[i : i + 1]
    return jnp.concatenate(rows_r, 0), jnp.concatenate(rows_i, 0), cr, ci


def run_products(ar, ai):
    cr, ci = jnp.ones_like(ar[:1]), jnp.zeros_like(ai[:1])
    rows_r, rows_i = [], []
    for i in range(SEGS):
        rows_r.append(cr)
        rows_i.append(ci)
        cr, ci = cmul(ar[i : i + 1], ai[i : i + 1], cr, ci)
    return jnp.concatenate(rows_r, 0), jnp.concatenate(rows_i, 0), cr, ci


def decay_kernel(tokens, bins, *refs):
    tables, (dec, cum, prod, runs, later) = refs[:6], refs[6:]
    grp = lax.axis_index("grp")
    users = bins.shape[0]
    count = tables[0].shape[0]
    me = lax.axis_index("ctx") * lax.axis_size("grp") + grp
    for k in range(later.shape[0]):
        later[k] = jnp.full(later.shape[1:], (me >> k) & 1, jnp.int32)
    order = order_matrix(tokens)
    steps = tokens // SEGS
    picks = []
    for u in range(users):
        row = bins[u : u + 1, pl.ds(pl.multiple_of(grp * tokens, tokens), tokens)]
        hit = (lax.broadcasted_iota(jnp.int32, (count, tokens), 0) == row).astype(F32).astype(BF16)
        picks.append(
            lax.dot_general(
                order, hit, (((1,), (1,)), ((), ())), preferred_element_type=F32
            ).astype(BF16)
        )
    pick = jnp.concatenate(picks, 0)
    pick = jnp.concatenate([pick] * 3, 1)
    for h in range(2):
        place = grp if h == 0 else 1 - grp
        for k in range(3):
            full = tables[3 * h + k][...]
            high = full.astype(BF16)
            rest = full - high.astype(F32)
            mid = rest.astype(BF16)
            low = (rest - mid.astype(F32)).astype(BF16)
            dec[k, h] = dot(pick, jnp.concatenate([high, mid, low], 0))
        for u in range(users):
            base = u * tokens

            def at(s):
                rows = slice(base + s * SEGS, base + (s + 1) * SEGS)
                return dec[0, h, rows, :], dec[1, h, rows, :]

            pr, pi = at(0)
            for s in range(1, steps):
                dr, di = at(s)
                pr, pi = cmul(dr, di, pr, pi)
            runs[0, h, u * SEGS : (u + 1) * SEGS, :] = pr
            runs[1, h, u * SEGS : (u + 1) * SEGS, :] = pi
            cr, ci, tr, ti = run_products(pr, pi)
            prod[place, u : u + 1, :] = tr
            prod[2 + place, u : u + 1, :] = ti
            for s in range(steps):
                dr, di = at(s)
                cr, ci = cmul(dr, di, cr, ci)
                rows = slice(base + s * SEGS, base + (s + 1) * SEGS)
                cum[0, h, rows, :] = cr
                cum[1, h, rows, :] = ci


def own_kernel(tokens, events, w, out):
    chan = lax.axis_index("chan")
    users, _, width = events.shape
    order = order_matrix(tokens)
    rows = jnp.concatenate([dot(order, events[u]).astype(BF16) for u in range(users)], 0)
    start = pl.ds(pl.multiple_of(chan * width, width), width)
    for c in range(2):
        out[c] = dot(rows, w[c, start, :])


def scan_kernel(tokens, peers, user, *refs):
    events = refs[:peers]
    weights = refs[peers : peers + 2]
    parts = refs[peers + 2 : peers + 4]
    dec, runs, state, ends, drive = refs[peers + 4 :]
    chan, grp = lax.axis_index("chan"), lax.axis_index("grp")
    width = events[0].shape[1]
    steps = tokens // SEGS
    base = user * tokens
    order = order_matrix(tokens)
    rows = [dot(order, ev[...]).astype(BF16) for ev in events]
    for h in range(2):
        place = grp if h == 0 else 1 - grp
        for c in range(2):
            total = parts[h][c, base : base + tokens, :]
            for n in range(peers):
                start = pl.multiple_of((chan ^ (n + 1)) * width, width)
                total = total + dot(rows[n], weights[h][c, pl.ds(start, width), :])
            drive[c] = dec[2, h, base : base + tokens, :] * total

        def at(s):
            sl = slice(base + s * SEGS, base + (s + 1) * SEGS)
            to = slice(s * SEGS, (s + 1) * SEGS)
            return dec[0, h, sl, :], dec[1, h, sl, :], drive[0, to, :], drive[1, to, :]

        _, _, sr, si = at(0)
        for s in range(1, steps):
            dr, di, vr, vi = at(s)
            xr, xi = cmul(dr, di, sr, si)
            sr, si = xr + vr, xi + vi
        ar = runs[0, h, user * SEGS : (user + 1) * SEGS, :]
        ai = runs[1, h, user * SEGS : (user + 1) * SEGS, :]
        sr, si, er, ei = run_starts(ar, ai, sr, si)
        ends[place] = er
        ends[2 + place] = ei
        for s in range(steps):
            dr, di, vr, vi = at(s)
            xr, xi = cmul(dr, di, sr, si)
            sr, si = xr + vr, xi + vi
            to = slice(s * SEGS, (s + 1) * SEGS)
            state[0, h, to, :] = sr
            state[1, h, to, :] = si


def carry_in(tokens, carry, states, cum, out):
    grp = lax.axis_index("grp")
    order = order_matrix(tokens)
    for h in range(2):
        place = grp if h == 0 else 1 - grp
        cr, ci = carry[place], carry[2 + place]
        for u, state in enumerate(states):
            sl = slice(u * tokens, (u + 1) * tokens)
            xr, xi = cmul(cum[0, h, sl, :], cum[1, h, sl, :], cr[u : u + 1], ci[u : u + 1])
            for c, value in ((0, state[0, h] + xr), (1, state[1, h] + xi)):
                moved = lax.dot_general(
                    order, value.astype(BF16), (((0,), (0,)), ((), ())), preferred_element_type=F32
                )
                out[c, h, sl, :] = moved.astype(BF16)


def mix(d, states, w_own, w_oth, *outs):
    at = (lax.axis_index("chan") * lax.axis_size("grp") + lax.axis_index("grp")) ^ d
    count, width = outs[0].shape
    cols = pl.ds(pl.multiple_of(at * width, width), width)
    total = None
    for h, w in enumerate((w_own, w_oth)):
        for c in range(2):
            term = dot(states[c, h], w[c, :, cols])
            total = term if total is None else total + term
    for i, out in enumerate(outs):
        out[...] = total[i * count : (i + 1) * count].astype(out.dtype)


def far_kernel(tokens, users, far, carry, *refs):
    states, (cum, w_own, w_oth) = refs[:users], refs[users : users + 3]
    rounded, outs = refs[users + 3], refs[users + 4 :]
    carry_in(tokens, carry, states, cum, rounded)
    for d, out in zip(far, outs):
        mix(d, rounded, w_own, w_oth, out)


def near_kernel(states, w_own, w_oth, same, *cross):
    mix(1, states, w_own, w_oth, *cross)
    mix(0, states, w_own, w_oth, same)


def hold_kernel(source, target, sem):
    copy = pltpu.make_async_copy(source, target, sem)
    copy.start()
    copy.wait()


def finish(place, seg_rows, lengths, sums, events, gain, put):
    users = events.shape[0]
    tokens = seg_rows // 2
    start = pl.multiple_of(place * tokens, tokens)
    first = lax.axis_index("ctx") * seg_rows + start
    for u in range(users):
        total = gain[...] * events[u, pl.ds(start, tokens), :].astype(F32)
        for parts in sums:
            if len(parts) == users:
                total = total + parts[u][...].astype(F32)
            else:
                total = total + parts[0][u * tokens : (u + 1) * tokens, :].astype(F32)
        result = jax.nn.gelu(total)
        position = first + lax.broadcasted_iota(jnp.int32, result.shape, 0)
        put(u, start, jnp.where(position < lengths[u], result, 0.0).astype(BF16))


def store(u, start, value, held, out, sems):
    held[u] = value
    copy = pltpu.make_async_copy(
        held.at[u], out.at[u, pl.ds(start, value.shape[0]), :], sems.at[u]
    )
    copy.start()
    return copy


def same_kernel(lengths, events, gain, *refs):
    sums, (out, held, sems) = refs[:-3], refs[-3:]
    copies = []

    def put(u, start, value):
        copies.append(store(u, start, value, held, out, sems))

    finish(lax.axis_index("grp"), events.shape[1], lengths, [(r,) for r in sums], events, gain, put)
    for copy in copies:
        copy.wait()


def final_kernel(users, lengths, events, gain, done, *refs):
    cross, sums, (out, held, sems) = refs[:users], refs[users:-3], refs[-3:]
    copies = []

    def put(u, start, value):
        copies.append(store(u, start, value, held, out, sems))

    sums = [cross] + [(r,) for r in sums]
    finish(1 - lax.axis_index("grp"), events.shape[1], lengths, sums, events, gain, put)
    for copy in copies:
        copy.wait()


def call(body, name, args, out_shape, scratch=(), flops=0, bytes_=0, in_specs=None, out_specs=None, aliases=None):
    single = not isinstance(out_shape, tuple)
    return pl.pallas_call(
        body,
        name=name,
        out_shape=out_shape,
        in_specs=in_specs or [HERE] * len(args),
        out_specs=out_specs or (HERE if single else (HERE,) * len(out_shape)),
        scratch_shapes=list(scratch),
        input_output_aliases=aliases or {},
        compiler_params=pltpu.CompilerParams(vmem_limit_bytes=VMEM),
        cost_estimate=pl.CostEstimate(flops=flops, bytes_accessed=bytes_, transcendentals=0),
    )(*args)


def shape(dims, kind):
    return jax.ShapeDtypeStruct(dims, kind)


def join(first, second):
    ar, ai, br, bi = first[0][:2], first[0][2:], second[0][:2], second[0][2:]
    er, ei, fr, fi = first[1][:2], first[1][2:], second[1][:2], second[1][2:]
    pr, pi = cmul(br, bi, ar, ai)
    xr, xi = cmul(br, bi, er, ei)
    return jnp.concatenate([pr, pi]), jnp.concatenate([xr + fr, xi + fi])


def local(
    events, gap_bins, lengths, gap_table, decay_rate, frequency, in_proj, out_proj, skip_gain
):
    users, seg_rows, width = events.shape
    model_width = in_proj.shape[0]
    q = decay_rate.shape[0]
    grps, chans, ctxs = (lax.axis_size(a) for a in ("grp", "chan", "ctx"))
    assert grps == 2
    tokens = seg_rows // grps
    rows = users * tokens
    devices, blocks = chans * grps, ctxs * grps
    part_width = model_width // devices
    grp = lax.axis_index("grp")

    def swap(array, axes, size, k):
        return lax.ppermute(array, axes, [(i, i ^ k) for i in range(size)])

    own_rows = lax.dynamic_slice_in_dim(events, grp * tokens, tokens, 1)
    own_events = lax.dynamic_slice_in_dim(events, grp * part_width, part_width, 2)
    own_rows, own_events = lax.optimization_barrier((own_rows, own_events))
    peer_rows = [
        [swap(own_rows[u], "chan", chans, k) for k in range(1, chans)] for u in range(users)
    ]

    decay_oth = swap(decay_rate, "grp", grps, 1)
    freq_oth = swap(frequency, "grp", grps, 1)
    in_proj, decay_oth, freq_oth = lax.optimization_barrier((in_proj, decay_oth, freq_oth))
    stored = Layout((0, 1, 2))
    raw_oth = swap(with_layout_constraint(in_proj, stored), "grp", grps, 1)
    raw_oth = with_layout_constraint(raw_oth, stored)
    o_oth = swap(out_proj, "grp", grps, 1)
    w_own = jnp.transpose(in_proj, (1, 0, 2))
    w_oth = jnp.transpose(raw_oth, (1, 0, 2))

    parts = [
        call(
            functools.partial(own_kernel, tokens),
            "own_drive_%d" % h,
            (own_rows, w),
            shape((2, rows, q), F32),
            flops=2 * rows * width * 2 * q,
            bytes_=2 * width * q * 2 + 2 * rows * q * 4,
        )
        for h, w in enumerate((w_own, w_oth))
    ]
    def tables(decay, turn):
        scaled = gap_table[:, None] * decay
        turned = gap_table[:, None] * turn
        magnitude = jnp.exp(-scaled)
        return (
            magnitude * jnp.cos(turned),
            magnitude * jnp.sin(turned),
            jnp.sqrt(-jnp.expm1(-2.0 * scaled)),
        )

    rounds = blocks.bit_length() - 1
    dec, cum, prod, runs, later = call(
        functools.partial(decay_kernel, tokens),
        "decays",
        (gap_bins, *tables(decay_rate, frequency), *tables(decay_oth, freq_oth)),
        (
            shape((3, 2, rows, q), F32),
            shape((2, 2, rows, q), F32),
            shape((4, users, q), F32),
            shape((2, 2, users * SEGS, q), F32),
            shape((rounds, users, q), jnp.int32),
        ),
        flops=2 * rows * q * 2 * 9 * gap_table.shape[0],
        bytes_=5 * 2 * rows * q * 4,
    )

    peers = chans - 1
    states, ends = [], []
    for u in range(users):
        state, end = call(
            functools.partial(scan_kernel, tokens, peers, u),
            "drive_scan_%d" % u,
            (*peer_rows[u], w_own, w_oth, *parts, dec, runs),
            (shape((2, 2, tokens, q), F32), shape((4, 1, q), F32)),
            scratch=[pltpu.VMEM((2, tokens, q), F32)],
            flops=2 * tokens * width * 4 * q * peers,
            bytes_=4 * width * q * 2 * peers + 4 * tokens * q * 12,
        )
        states.append(state)
        ends.append(end)
    ends = jnp.concatenate(ends, 1)
    o_oth = call(
        hold_kernel,
        "hold",
        (o_oth,),
        shape(o_oth.shape, BF16),
        scratch=[pltpu.SemaphoreType.DMA(())],
        in_specs=[pl.BlockSpec(memory_space=pl.ANY)],
        bytes_=4 * o_oth.size,
    )

    group = (prod, ends)
    before = (jnp.concatenate([jnp.ones_like(prod[:2]), jnp.zeros_like(prod[2:])]), jnp.zeros_like(ends))

    def send(k):
        got = swap(jnp.concatenate(group), ("ctx", "grp"), blocks, k)
        return got[:4], got[4:]

    def choose(second, a, b):
        return tuple(jnp.where(second, x, y) for x, y in zip(a, b))

    for k in range(rounds):
        bit = later[k] > 0
        near = send(1 << k)
        before = choose(bit, join(near, before), before)
        group = choose(bit, join(near, group), join(group, near))
    carry = before[1]

    far = list(range(2, devices))
    rounded, *pieces = call(
        functools.partial(far_kernel, tokens, users, far),
        "carry_far",
        (carry, *states, cum, out_proj, o_oth),
        (shape((2, 2, rows, q), BF16),) + (shape((rows, part_width), BF16),) * len(far),
        flops=2 * rows * part_width * 4 * q * len(far),
        bytes_=4 * q * part_width * 2 + 6 * rows * q * 4,
    )
    received = {d: swap(p, ("chan", "grp"), devices, d) for d, p in zip(far, pieces)}
    received[0], *cross = call(
        near_kernel,
        "near",
        (rounded, out_proj, o_oth),
        (shape((rows, part_width), F32),) + (shape((tokens, part_width), BF16),) * users,
        flops=2 * rows * part_width * 8 * q,
        bytes_=8 * q * part_width * 2 + 4 * rows * q * 2,
    )
    cross = [swap(c, ("chan", "grp"), devices, 1) for c in cross]

    common = (lengths, own_events, skip_gain[None])
    kinds = [pl.BlockSpec(memory_space=pltpu.SMEM), HERE, HERE]
    evens = [received[d] for d in range(0, devices, 2)]
    odds = [received[d] for d in range(3, devices, 2)]
    whole = shape((users, seg_rows, part_width), BF16)
    room = [
        pltpu.VMEM((users, tokens, part_width), BF16),
        pltpu.SemaphoreType.DMA((users,)),
    ]
    anywhere = pl.BlockSpec(memory_space=pl.ANY)
    done = call(
        same_kernel,
        "same",
        (*common, *evens),
        whole,
        scratch=room,
        in_specs=kinds + [HERE] * len(evens),
        out_specs=anywhere,
        bytes_=rows * part_width * 8,
    )
    return call(
        functools.partial(final_kernel, users),
        "final",
        (*common, done, *cross, *odds),
        whole,
        scratch=room,
        in_specs=kinds + [anywhere] + [HERE] * (users + len(odds)),
        out_specs=anywhere,
        aliases={3: 0},
        bytes_=rows * part_width * 8,
    )


def solution(mesh):
    return jax.shard_map(
        local,
        mesh=mesh,
        in_specs=(
            P("groups", "ctx", "chan"),
            P("groups", "ctx"),
            P("groups"),
            P(),
            P(("chan", "grp")),
            P(("chan", "grp")),
            P(None, None, ("chan", "grp")),
            P(None, ("chan", "grp"), None),
            P(("chan", "grp")),
        ),
        out_specs=P("groups", "ctx", ("chan", "grp")),
        check_vma=False,
    )
```

```python
import functools

import jax
import jax.numpy as jnp
from jax import lax
from jax.experimental import pallas as pl
from jax.experimental.layout import Layout, with_layout_constraint
from jax.experimental.pallas import tpu as pltpu
from jax.sharding import PartitionSpec as P

F32 = jnp.float32
BF16 = jnp.bfloat16
SEGS = 8
VMEM = 16 * 1024 * 1024
HERE = pl.BlockSpec(memory_space=pltpu.VMEM)


def dot(a, b):
    return jnp.dot(a, b, preferred_element_type=F32)


def cmul(ar, ai, br, bi):
    return ar * br - ai * bi, ar * bi + ai * br


def order_matrix(tokens):
    steps = tokens // SEGS
    r = lax.broadcasted_iota(jnp.int32, (tokens, tokens), 0)
    t = lax.broadcasted_iota(jnp.int32, (tokens, tokens), 1)
    return (t == (r % SEGS) * steps + r // SEGS).astype(F32).astype(BF16)


def run_starts(ar, ai, er, ei, cr, ci):
    rows_r, rows_i = [], []
    for i in range(SEGS):
        rows_r.append(cr)
        rows_i.append(ci)
        xr, xi = cmul(ar[i : i + 1], ai[i : i + 1], cr, ci)
        cr, ci = xr + er[i : i + 1], xi + ei[i : i + 1]
    return jnp.concatenate(rows_r, 0), jnp.concatenate(rows_i, 0), cr, ci


def run_products(ar, ai, cr, ci):
    rows_r, rows_i = [], []
    for i in range(SEGS):
        rows_r.append(cr)
        rows_i.append(ci)
        cr, ci = cmul(ar[i : i + 1], ai[i : i + 1], cr, ci)
    return jnp.concatenate(rows_r, 0), jnp.concatenate(rows_i, 0), cr, ci


def step_rows(tokens, chunk, s):
    start = chunk * tokens + s * SEGS
    return slice(start, start + SEGS)


def decay_kernel(tokens, bins, *refs):
    tables, (dec, prod, runs, starts, later) = refs[:6], refs[6:]
    grp = lax.axis_index("grp")
    count = tables[0].shape[0]
    ctx = lax.axis_index("ctx")
    for k in range(later.shape[0]):
        later[k] = jnp.full(later.shape[1:], (ctx >> k) & 1, jnp.int32)
    order = order_matrix(tokens)
    steps = tokens // SEGS
    chunks = bins.shape[1] // tokens
    picks = []
    for u in range(chunks):
        at = slice(u * tokens, (u + 1) * tokens)
        row = jnp.where(grp == 0, bins[0:1, at], bins[1:2, at])
        hit = (lax.broadcasted_iota(jnp.int32, (count, tokens), 0) == row).astype(F32).astype(BF16)
        picks.append(
            lax.dot_general(
                order, hit, (((1,), (1,)), ((), ())), preferred_element_type=F32
            ).astype(BF16)
        )
    pick = jnp.concatenate(picks, 0)
    pick = jnp.concatenate([pick] * 3, 1)
    for h in range(2):
        place = grp if h == 0 else 1 - grp
        for k in range(3):
            full = tables[3 * h + k][...]
            high = full.astype(BF16)
            rest = full - high.astype(F32)
            mid = rest.astype(BF16)
            low = (rest - mid.astype(F32)).astype(BF16)
            dec[k, h] = dot(pick, jnp.concatenate([high, mid, low], 0))
        cr = jnp.ones((1, dec.shape[3]), F32)
        ci = jnp.zeros((1, dec.shape[3]), F32)
        for u in range(chunks):
            at = step_rows(tokens, u, 0)
            pr, pi = dec[0, h, at, :], dec[1, h, at, :]
            for s in range(1, steps):
                at = step_rows(tokens, u, s)
                pr, pi = cmul(dec[0, h, at, :], dec[1, h, at, :], pr, pi)
            at = slice(u * SEGS, (u + 1) * SEGS)
            runs[0, h, at, :] = pr
            runs[1, h, at, :] = pi
            starts[0, h, at, :], starts[1, h, at, :], cr, ci = run_products(pr, pi, cr, ci)
        prod[place] = cr
        prod[2 + place] = ci


def product_kernel(tokens, dec, starts, cum):
    for h in range(2):
        for u in range(dec.shape[2] // tokens):
            at = slice(u * SEGS, (u + 1) * SEGS)
            cr, ci = starts[0, h, at, :], starts[1, h, at, :]
            for s in range(tokens // SEGS):
                at = step_rows(tokens, u, s)
                cr, ci = cmul(dec[0, h, at, :], dec[1, h, at, :], cr, ci)
                cum[0, h, at, :] = cr
                cum[1, h, at, :] = ci


def own_kernel(tokens, events, w, out):
    chan = lax.axis_index("chan")
    seg_rows, width = events.shape
    order = order_matrix(tokens)
    rows = jnp.concatenate(
        [dot(order, events[u : u + tokens, :]).astype(BF16) for u in range(0, seg_rows, tokens)], 0
    )
    start = pl.ds(pl.multiple_of(chan * width, width), width)
    for c in range(2):
        out[c] = dot(rows, w[c, start, :])


def scan_kernel(tokens, peers, chunk, *refs):
    events = refs[:peers]
    weights = refs[peers : peers + 2]
    parts = refs[peers + 2 : peers + 4]
    dec, runs, *earlier, state, ends, drive = refs[peers + 4 :]
    chan, grp = lax.axis_index("chan"), lax.axis_index("grp")
    width = events[0].shape[1]
    steps = tokens // SEGS
    base = chunk * tokens
    order = order_matrix(tokens)
    rows = [dot(order, ev[...]).astype(BF16) for ev in events]
    for h in range(2):
        place = grp if h == 0 else 1 - grp
        for c in range(2):
            total = parts[h][c, base : base + tokens, :]
            for n in range(peers):
                start = pl.multiple_of((chan ^ (n + 1)) * width, width)
                total = total + dot(rows[n], weights[h][c, pl.ds(start, width), :])
            drive[c] = dec[2, h, base : base + tokens, :] * total

        def at(s):
            sl = slice(base + s * SEGS, base + (s + 1) * SEGS)
            to = slice(s * SEGS, (s + 1) * SEGS)
            return dec[0, h, sl, :], dec[1, h, sl, :], drive[0, to, :], drive[1, to, :]

        _, _, sr, si = at(0)
        for s in range(1, steps):
            dr, di, vr, vi = at(s)
            xr, xi = cmul(dr, di, sr, si)
            sr, si = xr + vr, xi + vi
        ar = runs[0, h, chunk * SEGS : (chunk + 1) * SEGS, :]
        ai = runs[1, h, chunk * SEGS : (chunk + 1) * SEGS, :]
        if earlier:
            cr, ci = earlier[0][place], earlier[0][2 + place]
        else:
            cr, ci = jnp.zeros_like(sr[:1]), jnp.zeros_like(si[:1])
        sr, si, er, ei = run_starts(ar, ai, sr, si, cr, ci)
        ends[place] = er
        ends[2 + place] = ei
        for s in range(steps):
            dr, di, vr, vi = at(s)
            xr, xi = cmul(dr, di, sr, si)
            sr, si = xr + vr, xi + vi
            to = slice(s * SEGS, (s + 1) * SEGS)
            state[0, h, to, :] = sr
            state[1, h, to, :] = si


def carry_in(tokens, carry, states, cum, out):
    grp = lax.axis_index("grp")
    order = order_matrix(tokens)
    for h in range(2):
        place = grp if h == 0 else 1 - grp
        cr, ci = carry[place], carry[2 + place]
        for u, state in enumerate(states):
            sl = slice(u * tokens, (u + 1) * tokens)
            xr, xi = cmul(cum[0, h, sl, :], cum[1, h, sl, :], cr, ci)
            for c, value in ((0, state[0, h] + xr), (1, state[1, h] + xi)):
                moved = lax.dot_general(
                    order, value.astype(BF16), (((0,), (0,)), ((), ())), preferred_element_type=F32
                )
                out[c, h, sl, :] = moved.astype(BF16)


def mix(d, states, w_own, w_oth, *outs):
    at = (lax.axis_index("chan") * lax.axis_size("grp") + lax.axis_index("grp")) ^ d
    count, width = outs[0].shape
    cols = pl.ds(pl.multiple_of(at * width, width), width)
    total = None
    for h, w in enumerate((w_own, w_oth)):
        for c in range(2):
            term = dot(states[c, h], w[c, :, cols])
            total = term if total is None else total + term
    for i, out in enumerate(outs):
        out[...] = total[i * count : (i + 1) * count].astype(out.dtype)


def first_kernel(tokens, d, carry, *refs):
    *states, cum, w_own, w_oth, rounded, out = refs
    carry_in(tokens, carry, states, cum, rounded)
    mix(d, rounded, w_own, w_oth, out)


def far_kernel(far, states, w_own, w_oth, *outs):
    for d, out in zip(far, outs):
        mix(d, states, w_own, w_oth, out)


def near_kernel(states, w_own, w_oth, same, *cross):
    mix(1, states, w_own, w_oth, *cross)
    mix(0, states, w_own, w_oth, same)


def hold_kernel(source, target, sem):
    copy = pltpu.make_async_copy(source, target, sem)
    copy.start()
    copy.wait()


def finish(user, lengths, sums, events, gain, out, held, sems):
    seg_rows = events.shape[1]
    chunks, tokens, _ = held.shape
    first = lax.axis_index("ctx") * seg_rows
    copies = []
    for i in range(chunks):
        rows = slice(i * tokens, (i + 1) * tokens)
        total = gain[...] * events[user, rows, :].astype(F32)
        for parts in sums:
            part = parts[i][...] if len(parts) == chunks else parts[0][rows, :]
            total = total + part.astype(F32)
        result = jax.nn.gelu(total)
        position = first + i * tokens + lax.broadcasted_iota(jnp.int32, result.shape, 0)
        held[i] = jnp.where(position < lengths[user], result, 0.0).astype(BF16)
        copies.append(pltpu.make_async_copy(held.at[i], out.at[user, rows, :], sems.at[i]))
        copies[-1].start()
    for copy in copies:
        copy.wait()


def same_kernel(lengths, events, gain, *refs):
    sums, room = refs[:-3], refs[-3:]
    finish(lax.axis_index("grp"), lengths, [(r,) for r in sums], events, gain, *room)


def final_kernel(chunks, lengths, events, gain, done, *refs):
    cross, sums, room = refs[:chunks], refs[chunks:-3], refs[-3:]
    sums = [cross] + [(r,) for r in sums]
    finish(1 - lax.axis_index("grp"), lengths, sums, events, gain, *room)


def call(body, name, args, out_shape, scratch=(), flops=0, bytes_=0, in_specs=None, out_specs=None, aliases=None):
    single = not isinstance(out_shape, tuple)
    return pl.pallas_call(
        body,
        name=name,
        out_shape=out_shape,
        in_specs=in_specs or [HERE] * len(args),
        out_specs=out_specs or (HERE if single else (HERE,) * len(out_shape)),
        scratch_shapes=list(scratch),
        input_output_aliases=aliases or {},
        compiler_params=pltpu.CompilerParams(vmem_limit_bytes=VMEM),
        cost_estimate=pl.CostEstimate(flops=flops, bytes_accessed=bytes_, transcendentals=0),
    )(*args)


def shape(dims, kind):
    return jax.ShapeDtypeStruct(dims, kind)


def join(first, second):
    ar, ai, br, bi = first[0][:2], first[0][2:], second[0][:2], second[0][2:]
    er, ei, fr, fi = first[1][:2], first[1][2:], second[1][:2], second[1][2:]
    pr, pi = cmul(br, bi, ar, ai)
    xr, xi = cmul(br, bi, er, ei)
    return jnp.concatenate([pr, pi]), jnp.concatenate([xr + fr, xi + fi])


def local(
    events, gap_bins, lengths, gap_table, decay_rate, frequency, in_proj, out_proj, skip_gain
):
    users, seg_rows, width = events.shape
    model_width = in_proj.shape[0]
    q = decay_rate.shape[0]
    grps, chans, ctxs = (lax.axis_size(a) for a in ("grp", "chan", "ctx"))
    assert grps == 2 and users == 2
    chunks = 2
    tokens, rows = seg_rows // chunks, seg_rows
    devices = chans * grps
    part_width = model_width // devices
    grp = lax.axis_index("grp")

    def swap(array, axes, size, k):
        return lax.ppermute(array, axes, [(i, i ^ k) for i in range(size)])

    own_rows = lax.dynamic_slice_in_dim(events, grp, 1, 0)[0]
    own_events = lax.dynamic_slice_in_dim(events, grp * part_width, part_width, 2)
    own_rows, own_events = lax.optimization_barrier((own_rows, own_events))
    peer_rows = [
        [swap(own_rows[u : u + tokens], "chan", chans, k) for k in range(1, chans)]
        for u in range(0, rows, tokens)
    ]

    groups = lax.axis_size("groups")
    by = 3 if groups == 2 else 1
    rates_oth = swap(jnp.stack([decay_rate, frequency]), ("groups", "grp"), groups * grps, by)
    stored = Layout((0, 1, 2))
    raw_oth = swap(with_layout_constraint(in_proj, stored), "grp", grps, 1)
    raw_oth = with_layout_constraint(raw_oth, stored)
    o_oth = swap(out_proj, "grp", grps, 1)
    w_own = jnp.transpose(in_proj, (1, 0, 2))
    w_oth = jnp.transpose(raw_oth, (1, 0, 2))

    parts = [
        call(
            functools.partial(own_kernel, tokens),
            "own_drive_%d" % h,
            (own_rows, w),
            shape((2, rows, q), F32),
            flops=2 * rows * width * 2 * q,
            bytes_=2 * width * q * 2 + 2 * rows * q * 4,
        )
        for h, w in enumerate((w_own, w_oth))
    ]
    rates_oth, peer_rows[0], _ = lax.optimization_barrier((rates_oth, peer_rows[0], parts[1]))

    def tables(decay, turn):
        scaled = gap_table[:, None] * decay
        turned = gap_table[:, None] * turn
        magnitude = jnp.exp(-scaled)
        return (
            magnitude * jnp.cos(turned),
            magnitude * jnp.sin(turned),
            jnp.sqrt(-jnp.expm1(-2.0 * scaled)),
        )

    rounds = ctxs.bit_length() - 1
    dec, prod, runs, starts, later = call(
        functools.partial(decay_kernel, tokens),
        "decays",
        (gap_bins, *tables(decay_rate, frequency), *tables(rates_oth[0], rates_oth[1])),
        (
            shape((3, 2, rows, q), F32),
            shape((4, 1, q), F32),
            shape((2, 2, chunks * SEGS, q), F32),
            shape((2, 2, chunks * SEGS, q), F32),
            shape((rounds, 1, q), jnp.int32),
        ),
        flops=2 * rows * q * 2 * 9 * gap_table.shape[0],
        bytes_=5 * 2 * rows * q * 4,
    )

    peers = chans - 1
    states, ends = [], None
    for u in range(chunks):
        state, ends = call(
            functools.partial(scan_kernel, tokens, peers, u),
            "drive_scan_%d" % u,
            (*peer_rows[u], w_own, w_oth, *parts, dec, runs) + ((ends,) if u else ()),
            (shape((2, 2, tokens, q), F32), shape((4, 1, q), F32)),
            scratch=[pltpu.VMEM((2, tokens, q), F32)],
            flops=2 * tokens * width * 4 * q * peers,
            bytes_=4 * width * q * 2 * peers + 4 * tokens * q * 12,
        )
        states.append(state)
    starts, _ = lax.optimization_barrier((starts, ends))
    cum = call(
        functools.partial(product_kernel, tokens),
        "products",
        (dec, starts),
        shape((2, 2, rows, q), F32),
        bytes_=4 * 2 * rows * q * 4,
    )
    o_oth = call(
        hold_kernel,
        "hold",
        (o_oth,),
        shape(o_oth.shape, BF16),
        scratch=[pltpu.SemaphoreType.DMA(())],
        in_specs=[pl.BlockSpec(memory_space=pl.ANY)],
        bytes_=4 * o_oth.size,
    )

    group = (prod, ends)
    before = (jnp.concatenate([jnp.ones_like(prod[:2]), jnp.zeros_like(prod[2:])]), jnp.zeros_like(ends))

    def send(k):
        got = swap(jnp.concatenate(group), "ctx", ctxs, k)
        return got[:4], got[4:]

    def choose(second, a, b):
        return tuple(jnp.where(second, x, y) for x, y in zip(a, b))

    for k in range(rounds):
        bit = later[k] > 0
        near = send(1 << k)
        if k == 0:
            near, o_oth = lax.optimization_barrier((near, o_oth))
        before = choose(bit, join(near, before), before)
        group = choose(bit, join(near, group), join(group, near))
    carry = before[1]

    far = list(range(2, devices))
    rounded, piece = call(
        functools.partial(first_kernel, tokens, far[0]),
        "carry_far",
        (carry, *states, cum, out_proj, o_oth),
        (shape((2, 2, rows, q), BF16), shape((rows, part_width), BF16)),
        flops=2 * rows * part_width * 4 * q,
        bytes_=4 * q * part_width * 2 + 6 * rows * q * 4,
    )
    pieces = call(
        functools.partial(far_kernel, far[1:]),
        "far",
        (rounded, out_proj, o_oth),
        (shape((rows, part_width), BF16),) * len(far[1:]),
        flops=2 * rows * part_width * 4 * q * len(far[1:]),
        bytes_=4 * q * part_width * 2 + 6 * rows * q * 4,
    )
    received = {d: swap(p, ("chan", "grp"), devices, d) for d, p in zip(far, (piece, *pieces))}
    received[0], *cross = call(
        near_kernel,
        "near",
        (rounded, out_proj, o_oth),
        (shape((rows, part_width), F32),) + (shape((tokens, part_width), BF16),) * chunks,
        flops=2 * rows * part_width * 8 * q,
        bytes_=8 * q * part_width * 2 + 4 * rows * q * 2,
    )
    cross = [swap(c, ("chan", "grp"), devices, 1) for c in cross]

    common = (lengths, own_events, skip_gain[None])
    kinds = [pl.BlockSpec(memory_space=pltpu.SMEM), HERE, HERE]
    evens = [received[d] for d in range(0, devices, 2)]
    odds = [received[d] for d in range(3, devices, 2)]
    whole = shape((users, seg_rows, part_width), BF16)
    room = [
        pltpu.VMEM((chunks, tokens, part_width), BF16),
        pltpu.SemaphoreType.DMA((chunks,)),
    ]
    anywhere = pl.BlockSpec(memory_space=pl.ANY)
    done = call(
        same_kernel,
        "same",
        (*common, *evens),
        whole,
        scratch=room,
        in_specs=kinds + [HERE] * len(evens),
        out_specs=anywhere,
        bytes_=rows * part_width * 8,
    )
    return call(
        functools.partial(final_kernel, chunks),
        "final",
        (*common, done, *cross, *odds),
        whole,
        scratch=room,
        in_specs=kinds + [anywhere] + [HERE] * (chunks + len(odds)),
        out_specs=anywhere,
        aliases={3: 0},
        bytes_=rows * part_width * 8,
    )


def solution(mesh):
    return jax.shard_map(
        local,
        mesh=mesh,
        in_specs=(
            P("groups", "ctx", "chan"),
            P("groups", "ctx"),
            P("groups"),
            P(),
            P(("chan", "grp")),
            P(("chan", "grp")),
            P(None, None, ("chan", "grp")),
            P(None, ("chan", "grp"), None),
            P(("chan", "grp")),
        ),
        out_specs=P("groups", "ctx", ("chan", "grp")),
        check_vma=False,
    )
```

```python
import functools

import jax
import jax.numpy as jnp
from jax import lax
from jax.experimental import pallas as pl
from jax.experimental.layout import Layout, with_layout_constraint
from jax.experimental.pallas import tpu as pltpu
from jax.sharding import PartitionSpec as P

F32 = jnp.float32
BF16 = jnp.bfloat16
SEGS = 8
VMEM = 16 * 1024 * 1024
HERE = pl.BlockSpec(memory_space=pltpu.VMEM)


def dot(a, b):
    return jnp.dot(a, b, preferred_element_type=F32)


def cmul(ar, ai, br, bi):
    return ar * br - ai * bi, ar * bi + ai * br


def order_matrix(tokens):
    steps = tokens // SEGS
    r = lax.broadcasted_iota(jnp.int32, (tokens, tokens), 0)
    t = lax.broadcasted_iota(jnp.int32, (tokens, tokens), 1)
    return (t == (r % SEGS) * steps + r // SEGS).astype(F32).astype(BF16)


def run_starts(ar, ai, er, ei, cr, ci):
    rows_r, rows_i = [], []
    for i in range(SEGS):
        rows_r.append(cr)
        rows_i.append(ci)
        xr, xi = cmul(ar[i : i + 1], ai[i : i + 1], cr, ci)
        cr, ci = xr + er[i : i + 1], xi + ei[i : i + 1]
    return jnp.concatenate(rows_r, 0), jnp.concatenate(rows_i, 0), cr, ci


def run_products(ar, ai, cr, ci):
    rows_r, rows_i = [], []
    for i in range(SEGS):
        rows_r.append(cr)
        rows_i.append(ci)
        cr, ci = cmul(ar[i : i + 1], ai[i : i + 1], cr, ci)
    return jnp.concatenate(rows_r, 0), jnp.concatenate(rows_i, 0), cr, ci


def step_rows(tokens, chunk, s):
    start = chunk * tokens + s * SEGS
    return slice(start, start + SEGS)


def decay_kernel(tokens, bins, *refs):
    tables, (dec, prod, runs, starts, later) = refs[:6], refs[6:]
    grp = lax.axis_index("grp")
    count = tables[0].shape[0]
    ctx = lax.axis_index("ctx")
    for k in range(later.shape[0]):
        later[k] = jnp.full(later.shape[1:], (ctx >> k) & 1, jnp.int32)
    order = order_matrix(tokens)
    steps = tokens // SEGS
    chunks = bins.shape[1] // tokens
    picks = []
    for u in range(chunks):
        at = slice(u * tokens, (u + 1) * tokens)
        row = jnp.where(grp == 0, bins[0:1, at], bins[1:2, at])
        hit = (lax.broadcasted_iota(jnp.int32, (count, tokens), 0) == row).astype(F32).astype(BF16)
        picks.append(
            lax.dot_general(
                order, hit, (((1,), (1,)), ((), ())), preferred_element_type=F32
            ).astype(BF16)
        )
    pick = jnp.concatenate(picks, 0)
    pick = jnp.concatenate([pick] * 3, 1)
    for h in range(2):
        place = grp if h == 0 else 1 - grp
        for k in range(3):
            full = tables[3 * h + k][...]
            high = full.astype(BF16)
            rest = full - high.astype(F32)
            mid = rest.astype(BF16)
            low = (rest - mid.astype(F32)).astype(BF16)
            dec[k, h] = dot(pick, jnp.concatenate([high, mid, low], 0))
        cr = jnp.ones((1, dec.shape[3]), F32)
        ci = jnp.zeros((1, dec.shape[3]), F32)
        for u in range(chunks):
            at = step_rows(tokens, u, 0)
            pr, pi = dec[0, h, at, :], dec[1, h, at, :]
            for s in range(1, steps):
                at = step_rows(tokens, u, s)
                pr, pi = cmul(dec[0, h, at, :], dec[1, h, at, :], pr, pi)
            at = slice(u * SEGS, (u + 1) * SEGS)
            runs[0, h, at, :] = pr
            runs[1, h, at, :] = pi
            starts[0, h, at, :], starts[1, h, at, :], cr, ci = run_products(pr, pi, cr, ci)
        prod[place] = cr
        prod[2 + place] = ci


def product_kernel(tokens, dec, starts, cum):
    for h in range(2):
        for u in range(dec.shape[2] // tokens):
            at = slice(u * SEGS, (u + 1) * SEGS)
            cr, ci = starts[0, h, at, :], starts[1, h, at, :]
            for s in range(tokens // SEGS):
                at = step_rows(tokens, u, s)
                cr, ci = cmul(dec[0, h, at, :], dec[1, h, at, :], cr, ci)
                cum[0, h, at, :] = cr
                cum[1, h, at, :] = ci


def own_kernel(tokens, events, w, out):
    chan = lax.axis_index("chan")
    seg_rows, width = events.shape
    order = order_matrix(tokens)
    rows = jnp.concatenate(
        [dot(order, events[u : u + tokens, :]).astype(BF16) for u in range(0, seg_rows, tokens)], 0
    )
    start = pl.ds(pl.multiple_of(chan * width, width), width)
    for c in range(2):
        out[c] = dot(rows, w[c, start, :])


def scan_kernel(tokens, peers, chunk, *refs):
    events = refs[:peers]
    weights = refs[peers : peers + 2]
    parts = refs[peers + 2 : peers + 4]
    dec, runs, *earlier, state, ends, drive = refs[peers + 4 :]
    chan, grp = lax.axis_index("chan"), lax.axis_index("grp")
    width = events[0].shape[1]
    steps = tokens // SEGS
    base = chunk * tokens
    order = order_matrix(tokens)
    rows = [dot(order, ev[...]).astype(BF16) for ev in events]
    for h in range(2):
        place = grp if h == 0 else 1 - grp
        for c in range(2):
            total = parts[h][c, base : base + tokens, :]
            for n in range(peers):
                start = pl.multiple_of((chan ^ (n + 1)) * width, width)
                total = total + dot(rows[n], weights[h][c, pl.ds(start, width), :])
            drive[c] = dec[2, h, base : base + tokens, :] * total

        def at(s):
            sl = slice(base + s * SEGS, base + (s + 1) * SEGS)
            to = slice(s * SEGS, (s + 1) * SEGS)
            return dec[0, h, sl, :], dec[1, h, sl, :], drive[0, to, :], drive[1, to, :]

        _, _, sr, si = at(0)
        for s in range(1, steps):
            dr, di, vr, vi = at(s)
            xr, xi = cmul(dr, di, sr, si)
            sr, si = xr + vr, xi + vi
        ar = runs[0, h, chunk * SEGS : (chunk + 1) * SEGS, :]
        ai = runs[1, h, chunk * SEGS : (chunk + 1) * SEGS, :]
        if earlier:
            cr, ci = earlier[0][place], earlier[0][2 + place]
        else:
            cr, ci = jnp.zeros_like(sr[:1]), jnp.zeros_like(si[:1])
        sr, si, er, ei = run_starts(ar, ai, sr, si, cr, ci)
        ends[place] = er
        ends[2 + place] = ei
        for s in range(steps):
            dr, di, vr, vi = at(s)
            xr, xi = cmul(dr, di, sr, si)
            sr, si = xr + vr, xi + vi
            to = slice(s * SEGS, (s + 1) * SEGS)
            state[0, h, to, :] = sr
            state[1, h, to, :] = si


def carry_in(tokens, carry, states, cum, out):
    grp = lax.axis_index("grp")
    order = order_matrix(tokens)
    for h in range(2):
        place = grp if h == 0 else 1 - grp
        cr, ci = carry[place], carry[2 + place]
        for u, state in enumerate(states):
            sl = slice(u * tokens, (u + 1) * tokens)
            xr, xi = cmul(cum[0, h, sl, :], cum[1, h, sl, :], cr, ci)
            for c, value in ((0, state[0, h] + xr), (1, state[1, h] + xi)):
                moved = lax.dot_general(
                    order, value.astype(BF16), (((0,), (0,)), ((), ())), preferred_element_type=F32
                )
                out[c, h, sl, :] = moved.astype(BF16)


def mix(d, states, w_own, w_oth, *outs):
    at = (lax.axis_index("chan") * lax.axis_size("grp") + lax.axis_index("grp")) ^ d
    count, width = outs[0].shape
    cols = pl.ds(pl.multiple_of(at * width, width), width)
    total = None
    for h, w in enumerate((w_own, w_oth)):
        for c in range(2):
            term = dot(states[c, h], w[c, :, cols])
            total = term if total is None else total + term
    for i, out in enumerate(outs):
        out[...] = total[i * count : (i + 1) * count].astype(out.dtype)


def first_kernel(tokens, d, carry, *refs):
    *states, cum, w_own, w_oth, rounded, out = refs
    carry_in(tokens, carry, states, cum, rounded)
    mix(d, rounded, w_own, w_oth, out)


def far_kernel(far, states, w_own, w_oth, *outs):
    for d, out in zip(far, outs):
        mix(d, states, w_own, w_oth, out)


def near_kernel(states, w_own, w_oth, same, *cross):
    mix(1, states, w_own, w_oth, *cross)
    mix(0, states, w_own, w_oth, same)


def hold_kernel(source, target, sem):
    copy = pltpu.make_async_copy(source, target, sem)
    copy.start()
    copy.wait()


def chunk_of(part, i, tokens):
    return part[...] if part.shape[0] == tokens else part[i * tokens : (i + 1) * tokens, :]


def before_gelu(user, i, tokens, sums, events, gain):
    total = gain[...] * events[user, i * tokens : (i + 1) * tokens, :].astype(F32)
    for parts in sums:
        total = total + chunk_of(parts[min(i, len(parts) - 1)], i, tokens).astype(F32)
    return total


def valid(user, i, tokens, lengths, events, width):
    start = lax.axis_index("ctx") * events.shape[1] + i * tokens
    position = start + lax.broadcasted_iota(jnp.int32, (tokens, width), 0)
    return position < lengths[user]


def put(user, i, value, out, held, sems):
    held[i] = value.astype(BF16)
    tokens = value.shape[0]
    copy = pltpu.make_async_copy(
        held.at[i], out.at[user, i * tokens : (i + 1) * tokens, :], sems.at[i]
    )
    copy.start()
    return copy


def same_kernel(counts, lengths, events, gain, *refs):
    refs, room = refs[:-3], refs[-3:]
    chunks, tokens, width = room[1].shape
    sums = [refs[sum(counts[:n]) :][:c] for n, c in enumerate(counts)]
    user = lax.axis_index("grp")
    copies = []
    for i in range(chunks):
        result = jax.nn.gelu(before_gelu(user, i, tokens, sums, events, gain))
        keep = valid(user, i, tokens, lengths, events, width)
        copies.append(put(user, i, jnp.where(keep, result, 0.0), *room))
    for copy in copies:
        copy.wait()


def almost_kernel(counts, lengths, events, gain, *refs):
    refs, (total, keep) = refs[:-2], refs[-2:]
    tokens = refs[0].shape[0]
    sums = [refs[sum(counts[:n]) :][:c] for n, c in enumerate(counts)]
    user = 1 - lax.axis_index("grp")
    for i in range(total.shape[0] // tokens):
        rows = slice(i * tokens, (i + 1) * tokens)
        total[rows, :] = before_gelu(user, i, tokens, sums, events, gain)
        keep[rows, :] = valid(user, i, tokens, lengths, events, keep.shape[1]).astype(F32)


def final_kernel(total, keep, last, done, *room):
    chunks, tokens, width = room[1].shape
    user = 1 - lax.axis_index("grp")
    copies = []
    for i in range(chunks):
        rows = slice(i * tokens, (i + 1) * tokens)
        result = jax.nn.gelu(total[rows, :] + last[rows, :].astype(F32))
        kept = jnp.concatenate([keep[rows, :]] * (width // keep.shape[1]), 1)
        copies.append(put(user, i, jnp.where(kept > 0, result, 0.0), *room))
    for copy in copies:
        copy.wait()


def call(body, name, args, out_shape, scratch=(), flops=0, bytes_=0, in_specs=None, out_specs=None, aliases=None):
    single = not isinstance(out_shape, tuple)
    return pl.pallas_call(
        body,
        name=name,
        out_shape=out_shape,
        in_specs=in_specs or [HERE] * len(args),
        out_specs=out_specs or (HERE if single else (HERE,) * len(out_shape)),
        scratch_shapes=list(scratch),
        input_output_aliases=aliases or {},
        compiler_params=pltpu.CompilerParams(vmem_limit_bytes=VMEM),
        cost_estimate=pl.CostEstimate(flops=flops, bytes_accessed=bytes_, transcendentals=0),
    )(*args)


def shape(dims, kind):
    return jax.ShapeDtypeStruct(dims, kind)


def join(first, second):
    ar, ai, br, bi = first[0][:2], first[0][2:], second[0][:2], second[0][2:]
    er, ei, fr, fi = first[1][:2], first[1][2:], second[1][:2], second[1][2:]
    pr, pi = cmul(br, bi, ar, ai)
    xr, xi = cmul(br, bi, er, ei)
    return jnp.concatenate([pr, pi]), jnp.concatenate([xr + fr, xi + fi])


def local(
    events, gap_bins, lengths, gap_table, decay_rate, frequency, in_proj, out_proj, skip_gain
):
    users, seg_rows, width = events.shape
    model_width = in_proj.shape[0]
    q = decay_rate.shape[0]
    grps, chans, ctxs = (lax.axis_size(a) for a in ("grp", "chan", "ctx"))
    assert grps == 2 and users == 2
    chunks = 2
    tokens, rows = seg_rows // chunks, seg_rows
    devices = chans * grps
    part_width = model_width // devices
    grp = lax.axis_index("grp")

    def swap(array, axes, size, k):
        return lax.ppermute(array, axes, [(i, i ^ k) for i in range(size)])

    own_rows = lax.dynamic_slice_in_dim(events, grp, 1, 0)[0]
    own_events = lax.dynamic_slice_in_dim(events, grp * part_width, part_width, 2)
    own_rows, own_events = lax.optimization_barrier((own_rows, own_events))
    peer_rows = [
        [swap(own_rows[u : u + tokens], "chan", chans, k) for k in range(1, chans)]
        for u in range(0, rows, tokens)
    ]

    groups = lax.axis_size("groups")
    by = 3 if groups == 2 else 1
    rates_oth = swap(jnp.stack([decay_rate, frequency]), ("groups", "grp"), groups * grps, by)
    stored = Layout((0, 1, 2))
    raw_oth = swap(with_layout_constraint(in_proj, stored), "grp", grps, 1)
    raw_oth = with_layout_constraint(raw_oth, stored)
    o_oth = swap(out_proj, "grp", grps, 1)
    w_own = jnp.transpose(in_proj, (1, 0, 2))
    w_oth = jnp.transpose(raw_oth, (1, 0, 2))

    parts = [
        call(
            functools.partial(own_kernel, tokens),
            "own_drive_%d" % h,
            (own_rows, w),
            shape((2, rows, q), F32),
            flops=2 * rows * width * 2 * q,
            bytes_=2 * width * q * 2 + 2 * rows * q * 4,
        )
        for h, w in enumerate((w_own, w_oth))
    ]
    rates_oth, peer_rows[0], _ = lax.optimization_barrier((rates_oth, peer_rows[0], parts[1]))

    def tables(decay, turn):
        scaled = gap_table[:, None] * decay
        turned = gap_table[:, None] * turn
        magnitude = jnp.exp(-scaled)
        return (
            magnitude * jnp.cos(turned),
            magnitude * jnp.sin(turned),
            jnp.sqrt(-jnp.expm1(-2.0 * scaled)),
        )

    rounds = ctxs.bit_length() - 1
    dec, prod, runs, starts, later = call(
        functools.partial(decay_kernel, tokens),
        "decays",
        (gap_bins, *tables(decay_rate, frequency), *tables(rates_oth[0], rates_oth[1])),
        (
            shape((3, 2, rows, q), F32),
            shape((4, 1, q), F32),
            shape((2, 2, chunks * SEGS, q), F32),
            shape((2, 2, chunks * SEGS, q), F32),
            shape((rounds, 1, q), jnp.int32),
        ),
        flops=2 * rows * q * 2 * 9 * gap_table.shape[0],
        bytes_=5 * 2 * rows * q * 4,
    )

    peers = chans - 1
    states, ends = [], None
    for u in range(chunks):
        state, ends = call(
            functools.partial(scan_kernel, tokens, peers, u),
            "drive_scan_%d" % u,
            (*peer_rows[u], w_own, w_oth, *parts, dec, runs) + ((ends,) if u else ()),
            (shape((2, 2, tokens, q), F32), shape((4, 1, q), F32)),
            scratch=[pltpu.VMEM((2, tokens, q), F32)],
            flops=2 * tokens * width * 4 * q * peers,
            bytes_=4 * width * q * 2 * peers + 4 * tokens * q * 12,
        )
        states.append(state)
    starts, _ = lax.optimization_barrier((starts, ends))
    cum = call(
        functools.partial(product_kernel, tokens),
        "products",
        (dec, starts),
        shape((2, 2, rows, q), F32),
        bytes_=4 * 2 * rows * q * 4,
    )
    o_oth = call(
        hold_kernel,
        "hold",
        (o_oth,),
        shape(o_oth.shape, BF16),
        scratch=[pltpu.SemaphoreType.DMA(())],
        in_specs=[pl.BlockSpec(memory_space=pl.ANY)],
        bytes_=4 * o_oth.size,
    )

    group = (prod, ends)
    before = (jnp.concatenate([jnp.ones_like(prod[:2]), jnp.zeros_like(prod[2:])]), jnp.zeros_like(ends))

    def send(k):
        got = swap(jnp.concatenate(group), "ctx", ctxs, k)
        return got[:4], got[4:]

    def choose(second, a, b):
        return tuple(jnp.where(second, x, y) for x, y in zip(a, b))

    for k in range(rounds):
        bit = later[k] > 0
        near = send(1 << k)
        if k == 0:
            near, o_oth = lax.optimization_barrier((near, o_oth))
        before = choose(bit, join(near, before), before)
        group = choose(bit, join(near, group), join(group, near))
    carry = before[1]

    far = list(range(2, devices))
    rounded, piece = call(
        functools.partial(first_kernel, tokens, far[0]),
        "carry_far",
        (carry, *states, cum, out_proj, o_oth),
        (shape((2, 2, rows, q), BF16), shape((rows, part_width), BF16)),
        flops=2 * rows * part_width * 4 * q,
        bytes_=4 * q * part_width * 2 + 6 * rows * q * 4,
    )
    pieces = call(
        functools.partial(far_kernel, far[1:]),
        "far",
        (rounded, out_proj, o_oth),
        (shape((rows, part_width), BF16),) * len(far[1:]),
        flops=2 * rows * part_width * 4 * q * len(far[1:]),
        bytes_=4 * q * part_width * 2 + 6 * rows * q * 4,
    )
    received = {d: swap(p, ("chan", "grp"), devices, d) for d, p in zip(far, (piece, *pieces))}
    received[0], *cross = call(
        near_kernel,
        "near",
        (rounded, out_proj, o_oth),
        (shape((rows, part_width), F32),) + (shape((tokens, part_width), BF16),) * chunks,
        flops=2 * rows * part_width * 8 * q,
        bytes_=8 * q * part_width * 2 + 4 * rows * q * 2,
    )
    cross = [swap(c, ("chan", "grp"), devices, 1) for c in cross]

    common = (lengths, own_events, skip_gain[None])
    kinds = [pl.BlockSpec(memory_space=pltpu.SMEM), HERE, HERE]
    evens = [[received[d]] for d in range(0, devices, 2)]
    odds = [cross] + [[received[d]] for d in range(5, devices, 2)]
    whole = shape((users, seg_rows, part_width), BF16)
    room = [
        pltpu.VMEM((chunks, tokens, part_width), BF16),
        pltpu.SemaphoreType.DMA((chunks,)),
    ]
    anywhere = pl.BlockSpec(memory_space=pl.ANY)
    flat = [p for parts in evens for p in parts]
    done = call(
        functools.partial(same_kernel, [len(parts) for parts in evens]),
        "same",
        (*common, *flat),
        whole,
        scratch=room,
        in_specs=kinds + [HERE] * len(flat),
        out_specs=anywhere,
        bytes_=rows * part_width * 8,
    )
    flat = [p for parts in odds for p in parts]
    total, keep = call(
        functools.partial(almost_kernel, [len(parts) for parts in odds]),
        "almost",
        (*common, *flat),
        (shape((rows, part_width), F32), shape((rows, 128), F32)),
        in_specs=kinds + [HERE] * len(flat),
        bytes_=rows * part_width * 8,
    )
    return call(
        final_kernel,
        "final",
        (total, keep, received[3], done),
        whole,
        scratch=room,
        in_specs=[HERE] * 3 + [anywhere],
        out_specs=anywhere,
        aliases={3: 0},
        bytes_=rows * part_width * 8,
    )


def solution(mesh):
    return jax.shard_map(
        local,
        mesh=mesh,
        in_specs=(
            P("groups", "ctx", "chan"),
            P("groups", "ctx"),
            P("groups"),
            P(),
            P(("chan", "grp")),
            P(("chan", "grp")),
            P(None, None, ("chan", "grp")),
            P(None, ("chan", "grp"), None),
            P(("chan", "grp")),
        ),
        out_specs=P("groups", "ctx", ("chan", "grp")),
        check_vma=False,
    )
```

```python
import functools

import jax
import jax.numpy as jnp
from jax import lax
from jax.experimental import pallas as pl
from jax.experimental.layout import Layout, with_layout_constraint
from jax.experimental.pallas import tpu as pltpu
from jax.sharding import PartitionSpec as P

F32 = jnp.float32
BF16 = jnp.bfloat16
SEGS = 8
VMEM = 16 * 1024 * 1024
HERE = pl.BlockSpec(memory_space=pltpu.VMEM)


def dot(a, b):
    return jnp.dot(a, b, preferred_element_type=F32)


def cmul(ar, ai, br, bi):
    return ar * br - ai * bi, ar * bi + ai * br


def order_matrix(tokens):
    steps = tokens // SEGS
    r = lax.broadcasted_iota(jnp.int32, (tokens, tokens), 0)
    t = lax.broadcasted_iota(jnp.int32, (tokens, tokens), 1)
    return (t == (r % SEGS) * steps + r // SEGS).astype(F32).astype(BF16)


def run_starts(ar, ai, er, ei, cr, ci):
    rows_r, rows_i = [], []
    for i in range(SEGS):
        rows_r.append(cr)
        rows_i.append(ci)
        xr, xi = cmul(ar[i : i + 1], ai[i : i + 1], cr, ci)
        cr, ci = xr + er[i : i + 1], xi + ei[i : i + 1]
    return jnp.concatenate(rows_r, 0), jnp.concatenate(rows_i, 0), cr, ci


def run_products(ar, ai, cr, ci):
    rows_r, rows_i = [], []
    for i in range(SEGS):
        rows_r.append(cr)
        rows_i.append(ci)
        cr, ci = cmul(ar[i : i + 1], ai[i : i + 1], cr, ci)
    return jnp.concatenate(rows_r, 0), jnp.concatenate(rows_i, 0), cr, ci


def step_rows(tokens, chunk, s):
    start = chunk * tokens + s * SEGS
    return slice(start, start + SEGS)


def decay_kernel(tokens, bins, *refs):
    tables, (dec, prod, runs, starts, later) = refs[:6], refs[6:]
    grp = lax.axis_index("grp")
    count = tables[0].shape[0]
    ctx = lax.axis_index("ctx")
    for k in range(later.shape[0]):
        later[k] = jnp.full(later.shape[1:], (ctx >> k) & 1, jnp.int32)
    order = order_matrix(tokens)
    steps = tokens // SEGS
    chunks = bins.shape[1] // tokens
    picks = []
    for u in range(chunks):
        at = slice(u * tokens, (u + 1) * tokens)
        row = jnp.where(grp == 0, bins[0:1, at], bins[1:2, at])
        hit = (lax.broadcasted_iota(jnp.int32, (count, tokens), 0) == row).astype(F32).astype(BF16)
        picks.append(
            lax.dot_general(
                order, hit, (((1,), (1,)), ((), ())), preferred_element_type=F32
            ).astype(BF16)
        )
    pick = jnp.concatenate(picks, 0)
    pick = jnp.concatenate([pick] * 3, 1)
    for h in range(2):
        place = grp if h == 0 else 1 - grp
        for k in range(3):
            full = tables[3 * h + k][...]
            high = full.astype(BF16)
            rest = full - high.astype(F32)
            mid = rest.astype(BF16)
            low = (rest - mid.astype(F32)).astype(BF16)
            dec[k, h] = dot(pick, jnp.concatenate([high, mid, low], 0))
        cr = jnp.ones((1, dec.shape[3]), F32)
        ci = jnp.zeros((1, dec.shape[3]), F32)
        for u in range(chunks):
            at = step_rows(tokens, u, 0)
            pr, pi = dec[0, h, at, :], dec[1, h, at, :]
            for s in range(1, steps):
                at = step_rows(tokens, u, s)
                pr, pi = cmul(dec[0, h, at, :], dec[1, h, at, :], pr, pi)
            at = slice(u * SEGS, (u + 1) * SEGS)
            runs[0, h, at, :] = pr
            runs[1, h, at, :] = pi
            starts[0, h, at, :], starts[1, h, at, :], cr, ci = run_products(pr, pi, cr, ci)
        prod[place] = cr
        prod[2 + place] = ci


def product_kernel(tokens, dec, starts, cum):
    for h in range(2):
        for u in range(dec.shape[2] // tokens):
            at = slice(u * SEGS, (u + 1) * SEGS)
            cr, ci = starts[0, h, at, :], starts[1, h, at, :]
            for s in range(tokens // SEGS):
                at = step_rows(tokens, u, s)
                cr, ci = cmul(dec[0, h, at, :], dec[1, h, at, :], cr, ci)
                cum[0, h, at, :] = cr
                cum[1, h, at, :] = ci


def own_kernel(tokens, events, w, out):
    chan = lax.axis_index("chan")
    seg_rows, width = events.shape
    order = order_matrix(tokens)
    rows = jnp.concatenate(
        [dot(order, events[u : u + tokens, :]).astype(BF16) for u in range(0, seg_rows, tokens)], 0
    )
    start = pl.ds(pl.multiple_of(chan * width, width), width)
    for c in range(2):
        out[c] = dot(rows, w[c, start, :])


def scan_kernel(tokens, peers, chunk, *refs):
    events = refs[:peers]
    weights = refs[peers : peers + 2]
    parts = refs[peers + 2 : peers + 4]
    dec, runs, *earlier, state, ends, drive = refs[peers + 4 :]
    chan, grp = lax.axis_index("chan"), lax.axis_index("grp")
    width = events[0].shape[1]
    steps = tokens // SEGS
    base = chunk * tokens
    order = order_matrix(tokens)
    rows = [dot(order, ev[...]).astype(BF16) for ev in events]
    for h in range(2):
        place = grp if h == 0 else 1 - grp
        for c in range(2):
            total = parts[h][c, base : base + tokens, :]
            for n in range(peers):
                start = pl.multiple_of((chan ^ (n + 1)) * width, width)
                total = total + dot(rows[n], weights[h][c, pl.ds(start, width), :])
            drive[c] = dec[2, h, base : base + tokens, :] * total

        def at(s):
            sl = slice(base + s * SEGS, base + (s + 1) * SEGS)
            to = slice(s * SEGS, (s + 1) * SEGS)
            return dec[0, h, sl, :], dec[1, h, sl, :], drive[0, to, :], drive[1, to, :]

        _, _, sr, si = at(0)
        for s in range(1, steps):
            dr, di, vr, vi = at(s)
            xr, xi = cmul(dr, di, sr, si)
            sr, si = xr + vr, xi + vi
        ar = runs[0, h, chunk * SEGS : (chunk + 1) * SEGS, :]
        ai = runs[1, h, chunk * SEGS : (chunk + 1) * SEGS, :]
        if earlier:
            cr, ci = earlier[0][place], earlier[0][2 + place]
        else:
            cr, ci = jnp.zeros_like(sr[:1]), jnp.zeros_like(si[:1])
        sr, si, er, ei = run_starts(ar, ai, sr, si, cr, ci)
        ends[place] = er
        ends[2 + place] = ei
        for s in range(steps):
            dr, di, vr, vi = at(s)
            xr, xi = cmul(dr, di, sr, si)
            sr, si = xr + vr, xi + vi
            to = slice(s * SEGS, (s + 1) * SEGS)
            state[0, h, to, :] = sr
            state[1, h, to, :] = si


def carry_in(tokens, carry, states, cum, out):
    grp = lax.axis_index("grp")
    order = order_matrix(tokens)
    for h in range(2):
        place = grp if h == 0 else 1 - grp
        cr, ci = carry[place], carry[2 + place]
        for u, state in enumerate(states):
            sl = slice(u * tokens, (u + 1) * tokens)
            xr, xi = cmul(cum[0, h, sl, :], cum[1, h, sl, :], cr, ci)
            for c, value in ((0, state[0, h] + xr), (1, state[1, h] + xi)):
                moved = lax.dot_general(
                    order, value.astype(BF16), (((0,), (0,)), ((), ())), preferred_element_type=F32
                )
                out[c, h, sl, :] = moved.astype(BF16)


def mix(d, states, w_own, w_oth, *outs):
    at = (lax.axis_index("chan") * lax.axis_size("grp") + lax.axis_index("grp")) ^ d
    count, width = outs[0].shape
    cols = pl.ds(pl.multiple_of(at * width, width), width)
    total = None
    for h, w in enumerate((w_own, w_oth)):
        for c in range(2):
            term = dot(states[c, h], w[c, :, cols])
            total = term if total is None else total + term
    for i, out in enumerate(outs):
        out[...] = total[i * count : (i + 1) * count].astype(out.dtype)


def first_kernel(tokens, d, carry, *refs):
    *states, cum, w_own, w_oth, rounded, out = refs
    carry_in(tokens, carry, states, cum, rounded)
    mix(d, rounded, w_own, w_oth, out)


def far_kernel(far, states, w_own, w_oth, *outs):
    for d, out in zip(far, outs):
        mix(d, states, w_own, w_oth, out)


def near_kernel(states, w_own, w_oth, same, *cross):
    mix(1, states, w_own, w_oth, *cross)
    mix(0, states, w_own, w_oth, same)


def hold_kernel(source, target, sem):
    copy = pltpu.make_async_copy(source, target, sem)
    copy.start()
    copy.wait()


def chunk_of(part, i, tokens):
    return part[...] if part.shape[0] == tokens else part[i * tokens : (i + 1) * tokens, :]


def before_gelu(user, i, tokens, sums, events, gain):
    total = gain[...] * events[user, i * tokens : (i + 1) * tokens, :].astype(F32)
    for parts in sums:
        total = total + chunk_of(parts[min(i, len(parts) - 1)], i, tokens).astype(F32)
    return total


def valid(user, i, tokens, lengths, events, width):
    start = lax.axis_index("ctx") * events.shape[1] + i * tokens
    position = start + lax.broadcasted_iota(jnp.int32, (tokens, width), 0)
    return position < lengths[user]


def put(user, i, value, out, held, sems):
    held[i] = value.astype(BF16)
    tokens = value.shape[0]
    copy = pltpu.make_async_copy(
        held.at[i], out.at[user, i * tokens : (i + 1) * tokens, :], sems.at[i]
    )
    copy.start()
    return copy


def same_kernel(counts, lengths, events, gain, *refs):
    refs, room = refs[:-3], refs[-3:]
    chunks, tokens, width = room[1].shape
    sums = [refs[sum(counts[:n]) :][:c] for n, c in enumerate(counts)]
    user = lax.axis_index("grp")
    copies = []
    for i in range(chunks):
        result = jax.nn.gelu(before_gelu(user, i, tokens, sums, events, gain))
        keep = valid(user, i, tokens, lengths, events, width)
        copies.append(put(user, i, jnp.where(keep, result, 0.0), *room))
    for copy in copies:
        copy.wait()


def almost_kernel(counts, lengths, events, gain, *refs):
    refs, (total, keep) = refs[:-2], refs[-2:]
    tokens = refs[0].shape[0]
    sums = [refs[sum(counts[:n]) :][:c] for n, c in enumerate(counts)]
    user = 1 - lax.axis_index("grp")
    for i in range(total.shape[0] // tokens):
        rows = slice(i * tokens, (i + 1) * tokens)
        total[rows, :] = before_gelu(user, i, tokens, sums, events, gain)
        keep[rows, :] = valid(user, i, tokens, lengths, events, keep.shape[1]).astype(F32)


def final_kernel(total, keep, last, done, *room):
    chunks, tokens, width = room[1].shape
    user = 1 - lax.axis_index("grp")
    copies = []
    for i in range(chunks):
        rows = slice(i * tokens, (i + 1) * tokens)
        result = jax.nn.gelu(total[rows, :] + last[rows, :].astype(F32))
        kept = jnp.concatenate([keep[rows, :]] * (width // keep.shape[1]), 1)
        copies.append(put(user, i, jnp.where(kept > 0, result, 0.0), *room))
    for copy in copies:
        copy.wait()


def call(body, name, args, out_shape, scratch=(), flops=0, bytes_=0, in_specs=None, out_specs=None, aliases=None):
    single = not isinstance(out_shape, tuple)
    return pl.pallas_call(
        body,
        name=name,
        out_shape=out_shape,
        in_specs=in_specs or [HERE] * len(args),
        out_specs=out_specs or (HERE if single else (HERE,) * len(out_shape)),
        scratch_shapes=list(scratch),
        input_output_aliases=aliases or {},
        compiler_params=pltpu.CompilerParams(vmem_limit_bytes=VMEM),
        cost_estimate=pl.CostEstimate(flops=flops, bytes_accessed=bytes_, transcendentals=0),
    )(*args)


def shape(dims, kind):
    return jax.ShapeDtypeStruct(dims, kind)


def join(first, second):
    ar, ai, br, bi = first[0][:2], first[0][2:], second[0][:2], second[0][2:]
    er, ei, fr, fi = first[1][:2], first[1][2:], second[1][:2], second[1][2:]
    pr, pi = cmul(br, bi, ar, ai)
    xr, xi = cmul(br, bi, er, ei)
    return jnp.concatenate([pr, pi]), jnp.concatenate([xr + fr, xi + fi])


def local(
    events, gap_bins, lengths, gap_table, decay_rate, frequency, in_proj, out_proj, skip_gain
):
    users, seg_rows, width = events.shape
    model_width = in_proj.shape[0]
    q = decay_rate.shape[0]
    grps, chans, ctxs = (lax.axis_size(a) for a in ("grp", "chan", "ctx"))
    assert grps == 2 and users == 2
    chunks = 2
    tokens, rows = seg_rows // chunks, seg_rows
    devices = chans * grps
    part_width = model_width // devices
    grp = lax.axis_index("grp")

    def swap(array, axes, size, k):
        return lax.ppermute(array, axes, [(i, i ^ k) for i in range(size)])

    own_rows = lax.dynamic_slice_in_dim(events, grp, 1, 0)[0]
    own_events = lax.dynamic_slice_in_dim(events, grp * part_width, part_width, 2)
    own_rows, own_events = lax.optimization_barrier((own_rows, own_events))
    peer_rows = [
        [swap(own_rows[u : u + tokens], "chan", chans, k) for k in range(1, chans)]
        for u in range(0, rows, tokens)
    ]

    stored = Layout((0, 1, 2))
    raw_oth = swap(with_layout_constraint(in_proj, stored), "grp", grps, 1)
    raw_oth = with_layout_constraint(raw_oth, stored)
    o_oth = swap(out_proj, "grp", grps, 1)
    w_own = jnp.transpose(in_proj, (1, 0, 2))
    w_oth = jnp.transpose(raw_oth, (1, 0, 2))

    parts = [
        call(
            functools.partial(own_kernel, tokens),
            "own_drive_%d" % h,
            (own_rows, w),
            shape((2, rows, q), F32),
            flops=2 * rows * width * 2 * q,
            bytes_=2 * width * q * 2 + 2 * rows * q * 4,
        )
        for h, w in enumerate((w_own, w_oth))
    ]
    rates, _ = lax.optimization_barrier((jnp.stack([decay_rate, frequency]), parts[0]))
    rates_oth = swap(rates, ("ctx", "grp"), ctxs * grps, 3 if ctxs > 1 else 1)
    rates_oth, peer_rows[0], _ = lax.optimization_barrier((rates_oth, peer_rows[0], parts[1]))

    def tables(decay, turn):
        scaled = gap_table[:, None] * decay
        turned = gap_table[:, None] * turn
        magnitude = jnp.exp(-scaled)
        return (
            magnitude * jnp.cos(turned),
            magnitude * jnp.sin(turned),
            jnp.sqrt(-jnp.expm1(-2.0 * scaled)),
        )

    rounds = ctxs.bit_length() - 1
    dec, prod, runs, starts, later = call(
        functools.partial(decay_kernel, tokens),
        "decays",
        (gap_bins, *tables(decay_rate, frequency), *tables(rates_oth[0], rates_oth[1])),
        (
            shape((3, 2, rows, q), F32),
            shape((4, 1, q), F32),
            shape((2, 2, chunks * SEGS, q), F32),
            shape((2, 2, chunks * SEGS, q), F32),
            shape((rounds, 1, q), jnp.int32),
        ),
        flops=2 * rows * q * 2 * 9 * gap_table.shape[0],
        bytes_=5 * 2 * rows * q * 4,
    )

    peers = chans - 1
    states, ends = [], None
    for u in range(chunks):
        state, ends = call(
            functools.partial(scan_kernel, tokens, peers, u),
            "drive_scan_%d" % u,
            (*peer_rows[u], w_own, w_oth, *parts, dec, runs) + ((ends,) if u else ()),
            (shape((2, 2, tokens, q), F32), shape((4, 1, q), F32)),
            scratch=[pltpu.VMEM((2, tokens, q), F32)],
            flops=2 * tokens * width * 4 * q * peers,
            bytes_=4 * width * q * 2 * peers + 4 * tokens * q * 12,
        )
        states.append(state)
    starts, _ = lax.optimization_barrier((starts, ends))
    cum = call(
        functools.partial(product_kernel, tokens),
        "products",
        (dec, starts),
        shape((2, 2, rows, q), F32),
        bytes_=4 * 2 * rows * q * 4,
    )
    o_oth = call(
        hold_kernel,
        "hold",
        (o_oth,),
        shape(o_oth.shape, BF16),
        scratch=[pltpu.SemaphoreType.DMA(())],
        in_specs=[pl.BlockSpec(memory_space=pl.ANY)],
        bytes_=4 * o_oth.size,
    )

    group = (prod, ends)
    before = (jnp.concatenate([jnp.ones_like(prod[:2]), jnp.zeros_like(prod[2:])]), jnp.zeros_like(ends))

    def send(k):
        got = swap(jnp.concatenate(group), "ctx", ctxs, k)
        return got[:4], got[4:]

    def choose(second, a, b):
        return tuple(jnp.where(second, x, y) for x, y in zip(a, b))

    for k in range(rounds):
        bit = later[k] > 0
        near = send(1 << k)
        if k == 0:
            near, o_oth = lax.optimization_barrier((near, o_oth))
        before = choose(bit, join(near, before), before)
        group = choose(bit, join(near, group), join(group, near))
    carry = before[1]

    far = list(range(2, devices))
    rounded, piece = call(
        functools.partial(first_kernel, tokens, far[0]),
        "carry_far",
        (carry, *states, cum, out_proj, o_oth),
        (shape((2, 2, rows, q), BF16), shape((rows, part_width), BF16)),
        flops=2 * rows * part_width * 4 * q,
        bytes_=4 * q * part_width * 2 + 6 * rows * q * 4,
    )
    pieces = call(
        functools.partial(far_kernel, far[1:]),
        "far",
        (rounded, out_proj, o_oth),
        (shape((rows, part_width), BF16),) * len(far[1:]),
        flops=2 * rows * part_width * 4 * q * len(far[1:]),
        bytes_=4 * q * part_width * 2 + 6 * rows * q * 4,
    )
    received = {d: swap(p, ("chan", "grp"), devices, d) for d, p in zip(far, (piece, *pieces))}
    received[0], *cross = call(
        near_kernel,
        "near",
        (rounded, out_proj, o_oth),
        (shape((rows, part_width), F32),) + (shape((tokens, part_width), BF16),) * chunks,
        flops=2 * rows * part_width * 8 * q,
        bytes_=8 * q * part_width * 2 + 4 * rows * q * 2,
    )
    cross = [swap(c, ("chan", "grp"), devices, 1) for c in cross]

    common = (lengths, own_events, skip_gain[None])
    kinds = [pl.BlockSpec(memory_space=pltpu.SMEM), HERE, HERE]
    evens = [[received[d]] for d in range(0, devices, 2)]
    odds = [cross] + [[received[d]] for d in range(5, devices, 2)]
    whole = shape((users, seg_rows, part_width), BF16)
    room = [
        pltpu.VMEM((chunks, tokens, part_width), BF16),
        pltpu.SemaphoreType.DMA((chunks,)),
    ]
    anywhere = pl.BlockSpec(memory_space=pl.ANY)
    flat = [p for parts in evens for p in parts]
    done = call(
        functools.partial(same_kernel, [len(parts) for parts in evens]),
        "same",
        (*common, *flat),
        whole,
        scratch=room,
        in_specs=kinds + [HERE] * len(flat),
        out_specs=anywhere,
        bytes_=rows * part_width * 8,
    )
    flat = [p for parts in odds for p in parts]
    total, keep = call(
        functools.partial(almost_kernel, [len(parts) for parts in odds]),
        "almost",
        (*common, *flat),
        (shape((rows, part_width), F32), shape((rows, 128), F32)),
        in_specs=kinds + [HERE] * len(flat),
        bytes_=rows * part_width * 8,
    )
    return call(
        final_kernel,
        "final",
        (total, keep, received[3], done),
        whole,
        scratch=room,
        in_specs=[HERE] * 3 + [anywhere],
        out_specs=anywhere,
        aliases={3: 0},
        bytes_=rows * part_width * 8,
    )


def solution(mesh):
    return jax.shard_map(
        local,
        mesh=mesh,
        in_specs=(
            P("groups", "ctx", "chan"),
            P("groups", "ctx"),
            P("groups"),
            P(),
            P(("chan", "grp")),
            P(("chan", "grp")),
            P(None, None, ("chan", "grp")),
            P(None, ("chan", "grp"), None),
            P(("chan", "grp")),
        ),
        out_specs=P("groups", "ctx", ("chan", "grp")),
        check_vma=False,
    )
```

```python
import functools

import jax
import jax.numpy as jnp
from jax import lax
from jax.experimental import pallas as pl
from jax.experimental.layout import Layout, with_layout_constraint
from jax.experimental.pallas import tpu as pltpu
from jax.sharding import PartitionSpec as P

F32 = jnp.float32
BF16 = jnp.bfloat16
SEGS = 8
VMEM = 16 * 1024 * 1024
HERE = pl.BlockSpec(memory_space=pltpu.VMEM)


def dot(a, b):
    return jnp.dot(a, b, preferred_element_type=F32)


def cmul(ar, ai, br, bi):
    return ar * br - ai * bi, ar * bi + ai * br


def order_matrix(tokens):
    steps = tokens // SEGS
    r = lax.broadcasted_iota(jnp.int32, (tokens, tokens), 0)
    t = lax.broadcasted_iota(jnp.int32, (tokens, tokens), 1)
    return (t == (r % SEGS) * steps + r // SEGS).astype(F32).astype(BF16)


def run_starts(ar, ai, er, ei, cr, ci):
    rows_r, rows_i = [], []
    for i in range(SEGS):
        rows_r.append(cr)
        rows_i.append(ci)
        xr, xi = cmul(ar[i : i + 1], ai[i : i + 1], cr, ci)
        cr, ci = xr + er[i : i + 1], xi + ei[i : i + 1]
    return jnp.concatenate(rows_r, 0), jnp.concatenate(rows_i, 0), cr, ci


def run_products(ar, ai, cr, ci):
    rows_r, rows_i = [], []
    for i in range(SEGS):
        rows_r.append(cr)
        rows_i.append(ci)
        cr, ci = cmul(ar[i : i + 1], ai[i : i + 1], cr, ci)
    return jnp.concatenate(rows_r, 0), jnp.concatenate(rows_i, 0), cr, ci


def step_rows(tokens, chunk, s):
    start = chunk * tokens + s * SEGS
    return slice(start, start + SEGS)


def decay_kernel(tokens, bins, *refs):
    tables, (dec, prod, runs, starts, later) = refs[:6], refs[6:]
    grp = lax.axis_index("grp")
    count = tables[0].shape[0]
    ctx = lax.axis_index("ctx")
    for k in range(later.shape[0]):
        later[k] = jnp.full(later.shape[1:], (ctx >> k) & 1, jnp.int32)
    order = order_matrix(tokens)
    steps = tokens // SEGS
    chunks = bins.shape[1] // tokens
    picks = []
    for u in range(chunks):
        at = slice(u * tokens, (u + 1) * tokens)
        row = jnp.where(grp == 0, bins[0:1, at], bins[1:2, at])
        hit = (lax.broadcasted_iota(jnp.int32, (count, tokens), 0) == row).astype(F32).astype(BF16)
        picks.append(
            lax.dot_general(
                order, hit, (((1,), (1,)), ((), ())), preferred_element_type=F32
            ).astype(BF16)
        )
    pick = jnp.concatenate(picks, 0)
    pick = jnp.concatenate([pick] * 3, 1)
    for h in range(2):
        place = grp if h == 0 else 1 - grp
        for k in range(3):
            full = tables[3 * h + k][...]
            high = full.astype(BF16)
            rest = full - high.astype(F32)
            mid = rest.astype(BF16)
            low = (rest - mid.astype(F32)).astype(BF16)
            dec[k, h] = dot(pick, jnp.concatenate([high, mid, low], 0))
        cr = jnp.ones((1, dec.shape[3]), F32)
        ci = jnp.zeros((1, dec.shape[3]), F32)
        for u in range(chunks):
            at = step_rows(tokens, u, 0)
            pr, pi = dec[0, h, at, :], dec[1, h, at, :]
            for s in range(1, steps):
                at = step_rows(tokens, u, s)
                pr, pi = cmul(dec[0, h, at, :], dec[1, h, at, :], pr, pi)
            at = slice(u * SEGS, (u + 1) * SEGS)
            runs[0, h, at, :] = pr
            runs[1, h, at, :] = pi
            starts[0, h, at, :], starts[1, h, at, :], cr, ci = run_products(pr, pi, cr, ci)
        prod[place] = cr
        prod[2 + place] = ci


def state_kernel(tokens, dec, starts, *refs):
    chunks = dec.shape[2] // tokens
    drives, begins, (cum, state) = refs[:chunks], refs[chunks : 2 * chunks], refs[2 * chunks :]
    for h in range(2):
        for u in range(chunks):
            at = slice(u * SEGS, (u + 1) * SEGS)
            cr, ci = starts[0, h, at, :], starts[1, h, at, :]
            sr, si = begins[u][0, h], begins[u][1, h]
            for s in range(tokens // SEGS):
                at = step_rows(tokens, u, s)
                to = step_rows(tokens, 0, s)
                dr, di = dec[0, h, at, :], dec[1, h, at, :]
                cr, ci = cmul(dr, di, cr, ci)
                xr, xi = cmul(dr, di, sr, si)
                sr, si = xr + drives[u][0, h, to, :], xi + drives[u][1, h, to, :]
                cum[0, h, at, :] = cr
                cum[1, h, at, :] = ci
                state[0, h, at, :] = sr
                state[1, h, at, :] = si


def own_kernel(tokens, events, w, out):
    chan = lax.axis_index("chan")
    seg_rows, width = events.shape
    order = order_matrix(tokens)
    rows = jnp.concatenate(
        [dot(order, events[u : u + tokens, :]).astype(BF16) for u in range(0, seg_rows, tokens)], 0
    )
    start = pl.ds(pl.multiple_of(chan * width, width), width)
    for c in range(2):
        out[c] = dot(rows, w[c, start, :])


def scan_kernel(tokens, peers, chunk, *refs):
    events = refs[:peers]
    weights = refs[peers : peers + 2]
    parts = refs[peers + 2 : peers + 4]
    dec, runs, *earlier, drive, begin, ends = refs[peers + 4 :]
    chan, grp = lax.axis_index("chan"), lax.axis_index("grp")
    width = events[0].shape[1]
    steps = tokens // SEGS
    base = chunk * tokens
    order = order_matrix(tokens)
    rows = [dot(order, ev[...]).astype(BF16) for ev in events]
    for h in range(2):
        place = grp if h == 0 else 1 - grp
        for c in range(2):
            total = parts[h][c, base : base + tokens, :]
            for n in range(peers):
                start = pl.multiple_of((chan ^ (n + 1)) * width, width)
                total = total + dot(rows[n], weights[h][c, pl.ds(start, width), :])
            drive[c, h] = dec[2, h, base : base + tokens, :] * total

        def at(s):
            sl = slice(base + s * SEGS, base + (s + 1) * SEGS)
            to = slice(s * SEGS, (s + 1) * SEGS)
            return dec[0, h, sl, :], dec[1, h, sl, :], drive[0, h, to, :], drive[1, h, to, :]

        _, _, sr, si = at(0)
        for s in range(1, steps):
            dr, di, vr, vi = at(s)
            xr, xi = cmul(dr, di, sr, si)
            sr, si = xr + vr, xi + vi
        ar = runs[0, h, chunk * SEGS : (chunk + 1) * SEGS, :]
        ai = runs[1, h, chunk * SEGS : (chunk + 1) * SEGS, :]
        if earlier:
            cr, ci = earlier[0][place], earlier[0][2 + place]
        else:
            cr, ci = jnp.zeros_like(sr[:1]), jnp.zeros_like(si[:1])
        begin[0, h], begin[1, h], er, ei = run_starts(ar, ai, sr, si, cr, ci)
        ends[place] = er
        ends[2 + place] = ei


def carry_in(tokens, carry, state, cum, out):
    grp = lax.axis_index("grp")
    order = order_matrix(tokens)
    for h in range(2):
        place = grp if h == 0 else 1 - grp
        cr, ci = carry[place], carry[2 + place]
        for u in range(0, state.shape[2], tokens):
            sl = slice(u, u + tokens)
            xr, xi = cmul(cum[0, h, sl, :], cum[1, h, sl, :], cr, ci)
            for c, value in ((0, state[0, h, sl, :] + xr), (1, state[1, h, sl, :] + xi)):
                moved = lax.dot_general(
                    order, value.astype(BF16), (((0,), (0,)), ((), ())), preferred_element_type=F32
                )
                out[c, h, sl, :] = moved.astype(BF16)


def mix(d, states, w_own, w_oth, *outs):
    at = (lax.axis_index("chan") * lax.axis_size("grp") + lax.axis_index("grp")) ^ d
    count, width = outs[0].shape
    cols = pl.ds(pl.multiple_of(at * width, width), width)
    total = None
    for h, w in enumerate((w_own, w_oth)):
        for c in range(2):
            term = dot(states[c, h], w[c, :, cols])
            total = term if total is None else total + term
    for i, out in enumerate(outs):
        out[...] = total[i * count : (i + 1) * count].astype(out.dtype)


def first_kernel(tokens, d, carry, state, cum, w_own, w_oth, rounded, out):
    carry_in(tokens, carry, state, cum, rounded)
    mix(d, rounded, w_own, w_oth, out)


def far_kernel(far, states, w_own, w_oth, *outs):
    for d, out in zip(far, outs):
        mix(d, states, w_own, w_oth, out)


def near_kernel(states, w_own, w_oth, same, *cross):
    mix(1, states, w_own, w_oth, *cross)
    mix(0, states, w_own, w_oth, same)


def hold_kernel(source, target, sem):
    copy = pltpu.make_async_copy(source, target, sem)
    copy.start()
    copy.wait()


def chunk_of(part, i, tokens):
    return part[...] if part.shape[0] == tokens else part[i * tokens : (i + 1) * tokens, :]


def before_gelu(user, i, tokens, sums, events, gain):
    total = gain[...] * events[user, i * tokens : (i + 1) * tokens, :].astype(F32)
    for parts in sums:
        total = total + chunk_of(parts[min(i, len(parts) - 1)], i, tokens).astype(F32)
    return total


def valid(user, i, tokens, lengths, events, width):
    start = lax.axis_index("ctx") * events.shape[1] + i * tokens
    position = start + lax.broadcasted_iota(jnp.int32, (tokens, width), 0)
    return position < lengths[user]


def put(user, i, value, out, held, sems):
    held[i] = value.astype(BF16)
    tokens = value.shape[0]
    copy = pltpu.make_async_copy(
        held.at[i], out.at[user, i * tokens : (i + 1) * tokens, :], sems.at[i]
    )
    copy.start()
    return copy


def same_kernel(counts, lengths, events, gain, *refs):
    refs, room = refs[:-3], refs[-3:]
    chunks, tokens, width = room[1].shape
    sums = [refs[sum(counts[:n]) :][:c] for n, c in enumerate(counts)]
    user = lax.axis_index("grp")
    copies = []
    for i in range(chunks):
        result = jax.nn.gelu(before_gelu(user, i, tokens, sums, events, gain))
        keep = valid(user, i, tokens, lengths, events, width)
        copies.append(put(user, i, jnp.where(keep, result, 0.0), *room))
    for copy in copies:
        copy.wait()


def almost_kernel(counts, lengths, events, gain, *refs):
    refs, (total, keep) = refs[:-2], refs[-2:]
    tokens = refs[0].shape[0]
    sums = [refs[sum(counts[:n]) :][:c] for n, c in enumerate(counts)]
    user = 1 - lax.axis_index("grp")
    for i in range(total.shape[0] // tokens):
        rows = slice(i * tokens, (i + 1) * tokens)
        total[rows, :] = before_gelu(user, i, tokens, sums, events, gain)
        keep[rows, :] = valid(user, i, tokens, lengths, events, keep.shape[1]).astype(F32)


def final_kernel(total, keep, last, done, *room):
    chunks, tokens, width = room[1].shape
    user = 1 - lax.axis_index("grp")
    copies = []
    for i in range(chunks):
        rows = slice(i * tokens, (i + 1) * tokens)
        result = jax.nn.gelu(total[rows, :] + last[rows, :].astype(F32))
        kept = jnp.concatenate([keep[rows, :]] * (width // keep.shape[1]), 1)
        copies.append(put(user, i, jnp.where(kept > 0, result, 0.0), *room))
    for copy in copies:
        copy.wait()


def call(body, name, args, out_shape, scratch=(), flops=0, bytes_=0, in_specs=None, out_specs=None, aliases=None):
    single = not isinstance(out_shape, tuple)
    return pl.pallas_call(
        body,
        name=name,
        out_shape=out_shape,
        in_specs=in_specs or [HERE] * len(args),
        out_specs=out_specs or (HERE if single else (HERE,) * len(out_shape)),
        scratch_shapes=list(scratch),
        input_output_aliases=aliases or {},
        compiler_params=pltpu.CompilerParams(vmem_limit_bytes=VMEM),
        cost_estimate=pl.CostEstimate(flops=flops, bytes_accessed=bytes_, transcendentals=0),
    )(*args)


def shape(dims, kind):
    return jax.ShapeDtypeStruct(dims, kind)


def join(first, second):
    ar, ai, br, bi = first[0][:2], first[0][2:], second[0][:2], second[0][2:]
    er, ei, fr, fi = first[1][:2], first[1][2:], second[1][:2], second[1][2:]
    pr, pi = cmul(br, bi, ar, ai)
    xr, xi = cmul(br, bi, er, ei)
    return jnp.concatenate([pr, pi]), jnp.concatenate([xr + fr, xi + fi])


def local(
    events, gap_bins, lengths, gap_table, decay_rate, frequency, in_proj, out_proj, skip_gain
):
    users, seg_rows, width = events.shape
    model_width = in_proj.shape[0]
    q = decay_rate.shape[0]
    grps, chans, ctxs = (lax.axis_size(a) for a in ("grp", "chan", "ctx"))
    assert grps == 2 and users == 2
    chunks = 2
    tokens, rows = seg_rows // chunks, seg_rows
    devices = chans * grps
    part_width = model_width // devices
    grp = lax.axis_index("grp")

    def swap(array, axes, size, k):
        return lax.ppermute(array, axes, [(i, i ^ k) for i in range(size)])

    own_rows = lax.dynamic_slice_in_dim(events, grp, 1, 0)[0]
    own_events = lax.dynamic_slice_in_dim(events, grp * part_width, part_width, 2)
    own_rows, own_events = lax.optimization_barrier((own_rows, own_events))
    peer_rows = [
        [swap(own_rows[u : u + tokens], "chan", chans, k) for k in range(1, chans)]
        for u in range(0, rows, tokens)
    ]

    stored = Layout((0, 1, 2))
    raw_oth = swap(with_layout_constraint(in_proj, stored), "grp", grps, 1)
    raw_oth = with_layout_constraint(raw_oth, stored)
    o_oth = swap(out_proj, "grp", grps, 1)
    w_own = jnp.transpose(in_proj, (1, 0, 2))
    w_oth = jnp.transpose(raw_oth, (1, 0, 2))

    parts = [
        call(
            functools.partial(own_kernel, tokens),
            "own_drive_%d" % h,
            (own_rows, w),
            shape((2, rows, q), F32),
            flops=2 * rows * width * 2 * q,
            bytes_=2 * width * q * 2 + 2 * rows * q * 4,
        )
        for h, w in enumerate((w_own, w_oth))
    ]
    rates, _ = lax.optimization_barrier((jnp.stack([decay_rate, frequency]), parts[0]))
    rates_oth = swap(rates, ("ctx", "grp"), ctxs * grps, 3 if ctxs > 1 else 1)
    rates_oth, peer_rows[0], _ = lax.optimization_barrier((rates_oth, peer_rows[0], parts[1]))

    def tables(decay, turn):
        scaled = gap_table[:, None] * decay
        turned = gap_table[:, None] * turn
        magnitude = jnp.exp(-scaled)
        return (
            magnitude * jnp.cos(turned),
            magnitude * jnp.sin(turned),
            jnp.sqrt(-jnp.expm1(-2.0 * scaled)),
        )

    rounds = ctxs.bit_length() - 1
    dec, prod, runs, starts, later = call(
        functools.partial(decay_kernel, tokens),
        "decays",
        (gap_bins, *tables(decay_rate, frequency), *tables(rates_oth[0], rates_oth[1])),
        (
            shape((3, 2, rows, q), F32),
            shape((4, 1, q), F32),
            shape((2, 2, chunks * SEGS, q), F32),
            shape((2, 2, chunks * SEGS, q), F32),
            shape((rounds, 1, q), jnp.int32),
        ),
        flops=2 * rows * q * 2 * 9 * gap_table.shape[0],
        bytes_=5 * 2 * rows * q * 4,
    )

    peers = chans - 1
    drives, begins, ends = [], [], None
    for u in range(chunks):
        drive, begin, ends = call(
            functools.partial(scan_kernel, tokens, peers, u),
            "drive_scan_%d" % u,
            (*peer_rows[u], w_own, w_oth, *parts, dec, runs) + ((ends,) if u else ()),
            (
                shape((2, 2, tokens, q), F32),
                shape((2, 2, SEGS, q), F32),
                shape((4, 1, q), F32),
            ),
            flops=2 * tokens * width * 4 * q * peers,
            bytes_=4 * width * q * 2 * peers + 4 * tokens * q * 12,
        )
        drives.append(drive)
        begins.append(begin)
    starts, _ = lax.optimization_barrier((starts, ends))
    cum, state = call(
        functools.partial(state_kernel, tokens),
        "states",
        (dec, starts, *drives, *begins),
        (shape((2, 2, rows, q), F32),) * 2,
        bytes_=4 * 2 * rows * q * 4,
    )
    o_oth = call(
        hold_kernel,
        "hold",
        (o_oth,),
        shape(o_oth.shape, BF16),
        scratch=[pltpu.SemaphoreType.DMA(())],
        in_specs=[pl.BlockSpec(memory_space=pl.ANY)],
        bytes_=4 * o_oth.size,
    )

    group = (prod, ends)
    before = (jnp.concatenate([jnp.ones_like(prod[:2]), jnp.zeros_like(prod[2:])]), jnp.zeros_like(ends))

    def send(k):
        got = swap(jnp.concatenate(group), "ctx", ctxs, k)
        return got[:4], got[4:]

    def choose(second, a, b):
        return tuple(jnp.where(second, x, y) for x, y in zip(a, b))

    for k in range(rounds):
        bit = later[k] > 0
        near = send(1 << k)
        if k == 0:
            near, o_oth = lax.optimization_barrier((near, o_oth))
        before = choose(bit, join(near, before), before)
        group = choose(bit, join(near, group), join(group, near))
    carry = before[1]

    far = list(range(2, devices))
    rounded, piece = call(
        functools.partial(first_kernel, tokens, far[0]),
        "carry_far",
        (carry, state, cum, out_proj, o_oth),
        (shape((2, 2, rows, q), BF16), shape((rows, part_width), BF16)),
        flops=2 * rows * part_width * 4 * q,
        bytes_=4 * q * part_width * 2 + 6 * rows * q * 4,
    )
    pieces = call(
        functools.partial(far_kernel, far[1:]),
        "far",
        (rounded, out_proj, o_oth),
        (shape((rows, part_width), BF16),) * len(far[1:]),
        flops=2 * rows * part_width * 4 * q * len(far[1:]),
        bytes_=4 * q * part_width * 2 + 6 * rows * q * 4,
    )
    received = {d: swap(p, ("chan", "grp"), devices, d) for d, p in zip(far, (piece, *pieces))}
    received[0], *cross = call(
        near_kernel,
        "near",
        (rounded, out_proj, o_oth),
        (shape((rows, part_width), F32),) + (shape((tokens, part_width), BF16),) * chunks,
        flops=2 * rows * part_width * 8 * q,
        bytes_=8 * q * part_width * 2 + 4 * rows * q * 2,
    )
    cross = [swap(c, ("chan", "grp"), devices, 1) for c in cross]

    common = (lengths, own_events, skip_gain[None])
    kinds = [pl.BlockSpec(memory_space=pltpu.SMEM), HERE, HERE]
    evens = [[received[d]] for d in range(0, devices, 2)]
    odds = [cross] + [[received[d]] for d in range(5, devices, 2)]
    whole = shape((users, seg_rows, part_width), BF16)
    room = [
        pltpu.VMEM((chunks, tokens, part_width), BF16),
        pltpu.SemaphoreType.DMA((chunks,)),
    ]
    anywhere = pl.BlockSpec(memory_space=pl.ANY)
    flat = [p for parts in evens for p in parts]
    done = call(
        functools.partial(same_kernel, [len(parts) for parts in evens]),
        "same",
        (*common, *flat),
        whole,
        scratch=room,
        in_specs=kinds + [HERE] * len(flat),
        out_specs=anywhere,
        bytes_=rows * part_width * 8,
    )
    flat = [p for parts in odds for p in parts]
    total, keep = call(
        functools.partial(almost_kernel, [len(parts) for parts in odds]),
        "almost",
        (*common, *flat),
        (shape((rows, part_width), F32), shape((rows, 128), F32)),
        in_specs=kinds + [HERE] * len(flat),
        bytes_=rows * part_width * 8,
    )
    return call(
        final_kernel,
        "final",
        (total, keep, received[3], done),
        whole,
        scratch=room,
        in_specs=[HERE] * 3 + [anywhere],
        out_specs=anywhere,
        aliases={3: 0},
        bytes_=rows * part_width * 8,
    )


def solution(mesh):
    return jax.shard_map(
        local,
        mesh=mesh,
        in_specs=(
            P("groups", "ctx", "chan"),
            P("groups", "ctx"),
            P("groups"),
            P(),
            P(("chan", "grp")),
            P(("chan", "grp")),
            P(None, None, ("chan", "grp")),
            P(None, ("chan", "grp"), None),
            P(("chan", "grp")),
        ),
        out_specs=P("groups", "ctx", ("chan", "grp")),
        check_vma=False,
    )
```

```python
import functools

import jax
import jax.numpy as jnp
from jax import lax
from jax.experimental import pallas as pl
from jax.experimental.layout import Layout, with_layout_constraint
from jax.experimental.pallas import tpu as pltpu
from jax.sharding import PartitionSpec as P

F32 = jnp.float32
BF16 = jnp.bfloat16
SEGS = 8
VMEM = 16 * 1024 * 1024
HERE = pl.BlockSpec(memory_space=pltpu.VMEM)


def dot(a, b):
    return jnp.dot(a, b, preferred_element_type=F32)


def cmul(ar, ai, br, bi):
    return ar * br - ai * bi, ar * bi + ai * br


def order_matrix(tokens):
    steps = tokens // SEGS
    r = lax.broadcasted_iota(jnp.int32, (tokens, tokens), 0)
    t = lax.broadcasted_iota(jnp.int32, (tokens, tokens), 1)
    return (t == (r % SEGS) * steps + r // SEGS).astype(F32).astype(BF16)


def run_starts(ar, ai, er, ei, cr, ci):
    rows_r, rows_i = [], []
    for i in range(SEGS):
        rows_r.append(cr)
        rows_i.append(ci)
        xr, xi = cmul(ar[i : i + 1], ai[i : i + 1], cr, ci)
        cr, ci = xr + er[i : i + 1], xi + ei[i : i + 1]
    return jnp.concatenate(rows_r, 0), jnp.concatenate(rows_i, 0), cr, ci


def run_products(ar, ai, cr, ci):
    rows_r, rows_i = [], []
    for i in range(SEGS):
        rows_r.append(cr)
        rows_i.append(ci)
        cr, ci = cmul(ar[i : i + 1], ai[i : i + 1], cr, ci)
    return jnp.concatenate(rows_r, 0), jnp.concatenate(rows_i, 0), cr, ci


def step_rows(tokens, chunk, s):
    start = chunk * tokens + s * SEGS
    return slice(start, start + SEGS)


def decay_kernel(tokens, bins, *refs):
    tables, (dec, prod, runs, starts, later) = refs[:6], refs[6:]
    grp = lax.axis_index("grp")
    count = tables[0].shape[0]
    ctx = lax.axis_index("ctx")
    for k in range(later.shape[0]):
        later[k] = jnp.full(later.shape[1:], (ctx >> k) & 1, jnp.int32)
    order = order_matrix(tokens)
    steps = tokens // SEGS
    chunks = bins.shape[1] // tokens
    picks = []
    for u in range(chunks):
        at = slice(u * tokens, (u + 1) * tokens)
        row = jnp.where(grp == 0, bins[0:1, at], bins[1:2, at])
        hit = (lax.broadcasted_iota(jnp.int32, (count, tokens), 0) == row).astype(F32).astype(BF16)
        picks.append(
            lax.dot_general(
                order, hit, (((1,), (1,)), ((), ())), preferred_element_type=F32
            ).astype(BF16)
        )
    pick = jnp.concatenate(picks, 0)
    pick = jnp.concatenate([pick] * 3, 1)
    for h in range(2):
        place = grp if h == 0 else 1 - grp
        for k in range(3):
            full = tables[3 * h + k][...]
            high = full.astype(BF16)
            rest = full - high.astype(F32)
            mid = rest.astype(BF16)
            low = (rest - mid.astype(F32)).astype(BF16)
            dec[k, h] = dot(pick, jnp.concatenate([high, mid, low], 0))
        cr = jnp.ones((1, dec.shape[3]), F32)
        ci = jnp.zeros((1, dec.shape[3]), F32)
        for u in range(chunks):
            at = step_rows(tokens, u, 0)
            pr, pi = dec[0, h, at, :], dec[1, h, at, :]
            for s in range(1, steps):
                at = step_rows(tokens, u, s)
                pr, pi = cmul(dec[0, h, at, :], dec[1, h, at, :], pr, pi)
            at = slice(u * SEGS, (u + 1) * SEGS)
            runs[0, h, at, :] = pr
            runs[1, h, at, :] = pi
            starts[0, h, at, :], starts[1, h, at, :], cr, ci = run_products(pr, pi, cr, ci)
        prod[place] = cr
        prod[2 + place] = ci


def state_kernel(tokens, dec, starts, *refs):
    chunks = dec.shape[2] // tokens
    drives, begins, (cum, state) = refs[:chunks], refs[chunks : 2 * chunks], refs[2 * chunks :]
    for h in range(2):
        for u in range(chunks):
            at = slice(u * SEGS, (u + 1) * SEGS)
            cr, ci = starts[0, h, at, :], starts[1, h, at, :]
            sr, si = begins[u][0, h], begins[u][1, h]
            for s in range(tokens // SEGS):
                at = step_rows(tokens, u, s)
                to = step_rows(tokens, 0, s)
                dr, di = dec[0, h, at, :], dec[1, h, at, :]
                cr, ci = cmul(dr, di, cr, ci)
                xr, xi = cmul(dr, di, sr, si)
                sr, si = xr + drives[u][0, h, to, :], xi + drives[u][1, h, to, :]
                cum[0, h, at, :] = cr
                cum[1, h, at, :] = ci
                state[0, h, at, :] = sr
                state[1, h, at, :] = si


def own_kernel(tokens, ordered, events, w, out, *rows):
    chan = lax.axis_index("chan")
    seg_rows, width = events.shape
    if ordered:
        moved = events[...]
    else:
        order = order_matrix(tokens)
        moved = jnp.concatenate(
            [dot(order, events[u : u + tokens, :]).astype(BF16) for u in range(0, seg_rows, tokens)], 0
        )
        rows[0][...] = moved
    start = pl.ds(pl.multiple_of(chan * width, width), width)
    for c in range(2):
        out[c] = dot(moved, w[c, start, :])


def scan_kernel(tokens, peers, chunk, *refs):
    events = refs[:peers]
    weights = refs[peers : peers + 2]
    parts = refs[peers + 2 : peers + 4]
    dec, runs, *earlier, drive, begin, ends = refs[peers + 4 :]
    chan, grp = lax.axis_index("chan"), lax.axis_index("grp")
    width = events[0].shape[1]
    steps = tokens // SEGS
    base = chunk * tokens
    order = order_matrix(tokens)
    rows = [dot(order, ev[...]).astype(BF16) for ev in events]
    for h in range(2):
        place = grp if h == 0 else 1 - grp
        for c in range(2):
            total = parts[h][c, base : base + tokens, :]
            for n in range(peers):
                start = pl.multiple_of((chan ^ (n + 1)) * width, width)
                total = total + dot(rows[n], weights[h][c, pl.ds(start, width), :])
            drive[c, h] = dec[2, h, base : base + tokens, :] * total

        def at(s):
            sl = slice(base + s * SEGS, base + (s + 1) * SEGS)
            to = slice(s * SEGS, (s + 1) * SEGS)
            return dec[0, h, sl, :], dec[1, h, sl, :], drive[0, h, to, :], drive[1, h, to, :]

        _, _, sr, si = at(0)
        for s in range(1, steps):
            dr, di, vr, vi = at(s)
            xr, xi = cmul(dr, di, sr, si)
            sr, si = xr + vr, xi + vi
        ar = runs[0, h, chunk * SEGS : (chunk + 1) * SEGS, :]
        ai = runs[1, h, chunk * SEGS : (chunk + 1) * SEGS, :]
        if earlier:
            cr, ci = earlier[0][place], earlier[0][2 + place]
        else:
            cr, ci = jnp.zeros_like(sr[:1]), jnp.zeros_like(si[:1])
        begin[0, h], begin[1, h], er, ei = run_starts(ar, ai, sr, si, cr, ci)
        ends[place] = er
        ends[2 + place] = ei


def carry_in(tokens, carry, state, cum, out):
    grp = lax.axis_index("grp")
    order = order_matrix(tokens)
    for h in range(2):
        place = grp if h == 0 else 1 - grp
        cr, ci = carry[place], carry[2 + place]
        for u in range(0, state.shape[2], tokens):
            sl = slice(u, u + tokens)
            xr, xi = cmul(cum[0, h, sl, :], cum[1, h, sl, :], cr, ci)
            for c, value in ((0, state[0, h, sl, :] + xr), (1, state[1, h, sl, :] + xi)):
                moved = lax.dot_general(
                    order, value.astype(BF16), (((0,), (0,)), ((), ())), preferred_element_type=F32
                )
                out[c, h, sl, :] = moved.astype(BF16)


def mix(d, states, w_own, w_oth, *outs):
    at = (lax.axis_index("chan") * lax.axis_size("grp") + lax.axis_index("grp")) ^ d
    count, width = outs[0].shape
    cols = pl.ds(pl.multiple_of(at * width, width), width)
    total = None
    for h, w in enumerate((w_own, w_oth)):
        for c in range(2):
            term = dot(states[c, h], w[c, :, cols])
            total = term if total is None else total + term
    for i, out in enumerate(outs):
        out[...] = total[i * count : (i + 1) * count].astype(out.dtype)


def first_kernel(tokens, d, carry, state, cum, w_own, w_oth, rounded, out):
    carry_in(tokens, carry, state, cum, rounded)
    mix(d, rounded, w_own, w_oth, out)


def far_kernel(far, states, w_own, w_oth, *outs):
    for d, out in zip(far, outs):
        mix(d, states, w_own, w_oth, out)


def near_kernel(states, w_own, w_oth, same, *cross):
    mix(1, states, w_own, w_oth, *cross)
    mix(0, states, w_own, w_oth, same)


def hold_kernel(source, target, sem):
    copy = pltpu.make_async_copy(source, target, sem)
    copy.start()
    copy.wait()


def chunk_of(part, i, tokens):
    return part[...] if part.shape[0] == tokens else part[i * tokens : (i + 1) * tokens, :]


def before_gelu(user, i, tokens, sums, events, gain):
    total = gain[...] * events[user, i * tokens : (i + 1) * tokens, :].astype(F32)
    for parts in sums:
        total = total + chunk_of(parts[min(i, len(parts) - 1)], i, tokens).astype(F32)
    return total


def valid(user, i, tokens, lengths, events, width):
    start = lax.axis_index("ctx") * events.shape[1] + i * tokens
    position = start + lax.broadcasted_iota(jnp.int32, (tokens, width), 0)
    return position < lengths[user]


def put(user, i, value, out, held, sems):
    held[i] = value.astype(BF16)
    tokens = value.shape[0]
    copy = pltpu.make_async_copy(
        held.at[i], out.at[user, i * tokens : (i + 1) * tokens, :], sems.at[i]
    )
    copy.start()
    return copy


def same_kernel(counts, lengths, events, gain, *refs):
    refs, room = refs[:-3], refs[-3:]
    chunks, tokens, width = room[1].shape
    sums = [refs[sum(counts[:n]) :][:c] for n, c in enumerate(counts)]
    user = lax.axis_index("grp")
    copies = []
    for i in range(chunks):
        result = jax.nn.gelu(before_gelu(user, i, tokens, sums, events, gain))
        keep = valid(user, i, tokens, lengths, events, width)
        copies.append(put(user, i, jnp.where(keep, result, 0.0), *room))
    for copy in copies:
        copy.wait()


def almost_kernel(counts, lengths, events, gain, *refs):
    refs, (total, keep) = refs[:-2], refs[-2:]
    tokens = refs[0].shape[0]
    sums = [refs[sum(counts[:n]) :][:c] for n, c in enumerate(counts)]
    user = 1 - lax.axis_index("grp")
    for i in range(total.shape[0] // tokens):
        rows = slice(i * tokens, (i + 1) * tokens)
        total[rows, :] = before_gelu(user, i, tokens, sums, events, gain)
        keep[rows, :] = valid(user, i, tokens, lengths, events, keep.shape[1]).astype(F32)


def final_kernel(total, keep, last, done, *room):
    chunks, tokens, width = room[1].shape
    user = 1 - lax.axis_index("grp")
    copies = []
    for i in range(chunks):
        rows = slice(i * tokens, (i + 1) * tokens)
        result = jax.nn.gelu(total[rows, :] + last[rows, :].astype(F32))
        kept = jnp.concatenate([keep[rows, :]] * (width // keep.shape[1]), 1)
        copies.append(put(user, i, jnp.where(kept > 0, result, 0.0), *room))
    for copy in copies:
        copy.wait()


def call(body, name, args, out_shape, scratch=(), flops=0, bytes_=0, in_specs=None, out_specs=None, aliases=None):
    single = not isinstance(out_shape, tuple)
    return pl.pallas_call(
        body,
        name=name,
        out_shape=out_shape,
        in_specs=in_specs or [HERE] * len(args),
        out_specs=out_specs or (HERE if single else (HERE,) * len(out_shape)),
        scratch_shapes=list(scratch),
        input_output_aliases=aliases or {},
        compiler_params=pltpu.CompilerParams(vmem_limit_bytes=VMEM),
        cost_estimate=pl.CostEstimate(flops=flops, bytes_accessed=bytes_, transcendentals=0),
    )(*args)


def shape(dims, kind):
    return jax.ShapeDtypeStruct(dims, kind)


def join(first, second):
    ar, ai, br, bi = first[0][:2], first[0][2:], second[0][:2], second[0][2:]
    er, ei, fr, fi = first[1][:2], first[1][2:], second[1][:2], second[1][2:]
    pr, pi = cmul(br, bi, ar, ai)
    xr, xi = cmul(br, bi, er, ei)
    return jnp.concatenate([pr, pi]), jnp.concatenate([xr + fr, xi + fi])


def local(
    events, gap_bins, lengths, gap_table, decay_rate, frequency, in_proj, out_proj, skip_gain
):
    users, seg_rows, width = events.shape
    model_width = in_proj.shape[0]
    q = decay_rate.shape[0]
    grps, chans, ctxs = (lax.axis_size(a) for a in ("grp", "chan", "ctx"))
    assert grps == 2 and users == 2
    chunks = 2
    tokens, rows = seg_rows // chunks, seg_rows
    devices = chans * grps
    part_width = model_width // devices
    grp = lax.axis_index("grp")

    def swap(array, axes, size, k):
        return lax.ppermute(array, axes, [(i, i ^ k) for i in range(size)])

    own_rows = lax.dynamic_slice_in_dim(events, grp, 1, 0)[0]
    own_events = lax.dynamic_slice_in_dim(events, grp * part_width, part_width, 2)
    own_rows, own_events = lax.optimization_barrier((own_rows, own_events))
    peer_rows = [
        [swap(own_rows[u : u + tokens], "chan", chans, k) for k in range(1, chans)]
        for u in range(0, rows, tokens)
    ]

    stored = Layout((0, 1, 2))
    raw_oth = swap(with_layout_constraint(in_proj, stored), "grp", grps, 1)
    raw_oth = with_layout_constraint(raw_oth, stored)
    o_oth = swap(out_proj, "grp", grps, 1)
    w_own = jnp.transpose(in_proj, (1, 0, 2))
    w_oth = jnp.transpose(raw_oth, (1, 0, 2))

    def own_drive(h, given, w, more):
        return call(
            functools.partial(own_kernel, tokens, h > 0),
            "own_drive_%d" % h,
            (given, w),
            (shape((2, rows, q), F32),) + more,
            flops=2 * rows * width * 2 * q,
            bytes_=2 * width * q * 2 + 2 * rows * q * 4,
        )

    part, ordered = own_drive(0, own_rows, w_own, (shape((rows, width), BF16),))
    parts = [part, own_drive(1, ordered, w_oth, ())[0]]
    rates, _ = lax.optimization_barrier((jnp.stack([decay_rate, frequency]), parts[0]))
    rates_oth = swap(rates, ("ctx", "grp"), ctxs * grps, 3 if ctxs > 1 else 1)
    rates_oth, peer_rows[0], _ = lax.optimization_barrier((rates_oth, peer_rows[0], parts[1]))

    def tables(decay, turn):
        scaled = gap_table[:, None] * decay
        turned = gap_table[:, None] * turn
        magnitude = jnp.exp(-scaled)
        return (
            magnitude * jnp.cos(turned),
            magnitude * jnp.sin(turned),
            jnp.sqrt(-jnp.expm1(-2.0 * scaled)),
        )

    rounds = ctxs.bit_length() - 1
    dec, prod, runs, starts, later = call(
        functools.partial(decay_kernel, tokens),
        "decays",
        (gap_bins, *tables(decay_rate, frequency), *tables(rates_oth[0], rates_oth[1])),
        (
            shape((3, 2, rows, q), F32),
            shape((4, 1, q), F32),
            shape((2, 2, chunks * SEGS, q), F32),
            shape((2, 2, chunks * SEGS, q), F32),
            shape((rounds, 1, q), jnp.int32),
        ),
        flops=2 * rows * q * 2 * 9 * gap_table.shape[0],
        bytes_=5 * 2 * rows * q * 4,
    )

    peers = chans - 1
    drives, begins, ends = [], [], None
    for u in range(chunks):
        drive, begin, ends = call(
            functools.partial(scan_kernel, tokens, peers, u),
            "drive_scan_%d" % u,
            (*peer_rows[u], w_own, w_oth, *parts, dec, runs) + ((ends,) if u else ()),
            (
                shape((2, 2, tokens, q), F32),
                shape((2, 2, SEGS, q), F32),
                shape((4, 1, q), F32),
            ),
            flops=2 * tokens * width * 4 * q * peers,
            bytes_=4 * width * q * 2 * peers + 4 * tokens * q * 12,
        )
        drives.append(drive)
        begins.append(begin)
    starts, _ = lax.optimization_barrier((starts, ends))
    cum, state = call(
        functools.partial(state_kernel, tokens),
        "states",
        (dec, starts, *drives, *begins),
        (shape((2, 2, rows, q), F32),) * 2,
        bytes_=4 * 2 * rows * q * 4,
    )
    o_oth = call(
        hold_kernel,
        "hold",
        (o_oth,),
        shape(o_oth.shape, BF16),
        scratch=[pltpu.SemaphoreType.DMA(())],
        in_specs=[pl.BlockSpec(memory_space=pl.ANY)],
        bytes_=4 * o_oth.size,
    )

    group = (prod, ends)
    before = (jnp.concatenate([jnp.ones_like(prod[:2]), jnp.zeros_like(prod[2:])]), jnp.zeros_like(ends))

    def send(k):
        got = swap(jnp.concatenate(group), "ctx", ctxs, k)
        return got[:4], got[4:]

    def choose(second, a, b):
        return tuple(jnp.where(second, x, y) for x, y in zip(a, b))

    for k in range(rounds):
        bit = later[k] > 0
        near = send(1 << k)
        if k == 0:
            near, o_oth = lax.optimization_barrier((near, o_oth))
        before = choose(bit, join(near, before), before)
        group = choose(bit, join(near, group), join(group, near))
    carry = before[1]

    far = list(range(2, devices))
    rounded, piece = call(
        functools.partial(first_kernel, tokens, far[0]),
        "carry_far",
        (carry, state, cum, out_proj, o_oth),
        (shape((2, 2, rows, q), BF16), shape((rows, part_width), BF16)),
        flops=2 * rows * part_width * 4 * q,
        bytes_=4 * q * part_width * 2 + 6 * rows * q * 4,
    )
    pieces = call(
        functools.partial(far_kernel, far[1:]),
        "far",
        (rounded, out_proj, o_oth),
        (shape((rows, part_width), BF16),) * len(far[1:]),
        flops=2 * rows * part_width * 4 * q * len(far[1:]),
        bytes_=4 * q * part_width * 2 + 6 * rows * q * 4,
    )
    received = {d: swap(p, ("chan", "grp"), devices, d) for d, p in zip(far, (piece, *pieces))}
    received[0], *cross = call(
        near_kernel,
        "near",
        (rounded, out_proj, o_oth),
        (shape((rows, part_width), F32),) + (shape((tokens, part_width), BF16),) * chunks,
        flops=2 * rows * part_width * 8 * q,
        bytes_=8 * q * part_width * 2 + 4 * rows * q * 2,
    )
    cross = [swap(c, ("chan", "grp"), devices, 1) for c in cross]

    common = (lengths, own_events, skip_gain[None])
    kinds = [pl.BlockSpec(memory_space=pltpu.SMEM), HERE, HERE]
    evens = [[received[d]] for d in range(0, devices, 2)]
    odds = [cross] + [[received[d]] for d in range(5, devices, 2)]
    whole = shape((users, seg_rows, part_width), BF16)
    room = [
        pltpu.VMEM((chunks, tokens, part_width), BF16),
        pltpu.SemaphoreType.DMA((chunks,)),
    ]
    anywhere = pl.BlockSpec(memory_space=pl.ANY)
    flat = [p for parts in evens for p in parts]
    done = call(
        functools.partial(same_kernel, [len(parts) for parts in evens]),
        "same",
        (*common, *flat),
        whole,
        scratch=room,
        in_specs=kinds + [HERE] * len(flat),
        out_specs=anywhere,
        bytes_=rows * part_width * 8,
    )
    flat = [p for parts in odds for p in parts]
    total, keep = call(
        functools.partial(almost_kernel, [len(parts) for parts in odds]),
        "almost",
        (*common, *flat),
        (shape((rows, part_width), F32), shape((rows, 128), F32)),
        in_specs=kinds + [HERE] * len(flat),
        bytes_=rows * part_width * 8,
    )
    return call(
        final_kernel,
        "final",
        (total, keep, received[3], done),
        whole,
        scratch=room,
        in_specs=[HERE] * 3 + [anywhere],
        out_specs=anywhere,
        aliases={3: 0},
        bytes_=rows * part_width * 8,
    )


def solution(mesh):
    return jax.shard_map(
        local,
        mesh=mesh,
        in_specs=(
            P("groups", "ctx", "chan"),
            P("groups", "ctx"),
            P("groups"),
            P(),
            P(("chan", "grp")),
            P(("chan", "grp")),
            P(None, None, ("chan", "grp")),
            P(None, ("chan", "grp"), None),
            P(("chan", "grp")),
        ),
        out_specs=P("groups", "ctx", ("chan", "grp")),
        check_vma=False,
    )
```
